32 devices in a mesh: dp: 4 (over z), row: 2 (over core), col: 4 (over y, x).
Axes of the slice: x: 2, y: 2, z: 4, core: 2. Of those that a mesh axis runs over, the one named last changes fastest.
Arguments:
- tokens: bfloat16 [8192, 1024], P(('dp', 'row'), 'col'), may hold values from -6 to 6
- segment_ids: int32 [4, 2048], P('dp'), may hold values from 0 to 7, as said below
- cotangent: bfloat16 [8192, 1024], P(('dp', 'row'), 'col'), may hold values from -6 to 6
- qkv_weight: bfloat16 [1024, 3, 16, 64], P('col', None, 'row'), may hold values from -0.1875 to 0.1875
- attn_weight: bfloat16 [16, 64, 1024], P('row', None, 'col'), may hold values from -1 to 1
- in_weight: bfloat16 [1024, 2, 2624], P('col', None, 'row'), may hold values from -0.1875 to 0.1875
- out_weight: bfloat16 [2624, 1024], P('row', 'col'), may hold values from -0.125 to 0.125
- norm_gains: float32 [2, 1024], P(None, 'col'), may hold values from 0.4 to 3
- qkv_master: float32 [1024, 3, 16, 64], P(('col', 'dp'), None, 'row'), may hold values from -0.1875 to 0.1875
- attn_master: float32 [16, 64, 1024], P('row', None, ('col', 'dp')), may hold values from -0.1875 to 0.1875
- in_master: float32 [1024, 2, 2624], P(('col', 'dp'), None, 'row'), may hold values from -0.1875 to 0.1875
- out_master: float32 [2624, 1024], P('row', ('col', 'dp')), may hold values from -0.125 to 0.125
- qkv_first: float32 [1024, 3, 16, 64], P(('col', 'dp'), None, 'row'), may hold values from -0.00048828125 to 0.00048828125
- attn_first: float32 [16, 64, 1024], P('row', None, ('col', 'dp')), may hold values from -0.00048828125 to 0.00048828125
- in_first: float32 [1024, 2, 2624], P(('col', 'dp'), None, 'row'), may hold values from -0.00048828125 to 0.00048828125
- out_first: float32 [2624, 1024], P('row', ('col', 'dp')), may hold values from -0.00048828125 to 0.00048828125
- qkv_second: float32 [1024, 3, 16, 64], P(('col', 'dp'), None, 'row'), may hold values from 8.1584167e-10 to 1.3053467e-08
- attn_second: float32 [16, 64, 1024], P('row', None, ('col', 'dp')), may hold values from 3.2633668e-10 to 3.2633667e-09
- in_second: float32 [1024, 2, 2624], P(('col', 'dp'), None, 'row'), may hold values from 8.1584167e-10 to 1.3053467e-08
- out_second: float32 [2624, 1024], P('row', ('col', 'dp')), may hold values from 8.1584167e-10 to 1.3053467e-08
- gains_first: float32 [2, 1024], P(None, 'col'), may hold values from -0.00048828125 to 0.00048828125
- gains_second: float32 [2, 1024], P(None, 'col'), may hold values from 8.1584167e-10 to 1.3053467e-08
Outputs:
- layer_out: bfloat16 [8192, 1024], P(('dp', 'row'), 'col')
- input_grad: float32 [8192, 1024], P(('dp', 'row'), 'col')
- grad_norm: float32 [], replicated
- new_qkv_first: float32 [1024, 3, 16, 64], P(('col', 'dp'), None, 'row')
- new_attn_first: float32 [16, 64, 1024], P('row', None, ('col', 'dp'))
- new_in_first: float32 [1024, 2, 2624], P(('col', 'dp'), None, 'row')
- new_out_first: float32 [2624, 1024], P('row', ('col', 'dp'))
- new_qkv_second: float32 [1024, 3, 16, 64], P(('col', 'dp'), None, 'row')
- new_attn_second: float32 [16, 64, 1024], P('row', None, ('col', 'dp'))
- new_in_second: float32 [1024, 2, 2624], P(('col', 'dp'), None, 'row')
- new_out_second: float32 [2624, 1024], P('row', ('col', 'dp'))
- new_qkv_master: float32 [1024, 3, 16, 64], P(('col', 'dp'), None, 'row')
- new_attn_master: float32 [16, 64, 1024], P('row', None, ('col', 'dp'))
- new_in_master: float32 [1024, 2, 2624], P(('col', 'dp'), None, 'row')
- new_out_master: float32 [2624, 1024], P('row', ('col', 'dp'))
- new_qkv_copy: bfloat16 [1024, 3, 16, 64], P(('col', 'dp'), None, 'row')
- new_attn_copy: bfloat16 [16, 64, 1024], P('row', None, ('col', 'dp'))
- new_in_copy: bfloat16 [1024, 2, 2624], P(('col', 'dp'), None, 'row')
- new_out_copy: bfloat16 [2624, 1024], P('row', ('col', 'dp'))
- new_gains_first: float32 [2, 1024], P(None, 'col')
- new_gains_second: float32 [2, 1024], P(None, 'col')
- new_gains: float32 [2, 1024], P(None, 'col')
The draws below stay inside these ranges and needn't reach their ends.
Inputs may be any that keep to these rules, and one draw needn't show every extreme that they name: `segment_ids`: along each sequence the ids never fall; the first position has id 0 and the last 7, and ids may skip values; the positions p with 3/8 * 2048 <= p < 5/8 * 2048 of each sequence lie in one document.
All inputs are finite; a program needn't handle non-finite values.
Results may differ from the reference program's by a relative error of at most 0.024.
Values may be sent and summed in bfloat16 or wider, within the bound.
No kernel may reach another device: no remote copies, remote signals or barrier semaphores. Data moves between devices by JAX's collectives and lax.ppermute only.
A program may use at most 192 MiB of HBM per device.

```python
import math
import jax
import jax.numpy as jnp
from jax import lax

D = 1024
H = 16
HD = 64
FF = 2624
SEQ_LEN = 2048
DOCS = 8
STEP = 10
SEQS = 4
TOKENS = 8192
FEAT_COL = 256
PARAMS = 12257280


def rising(growth):
    place_index = jnp.arange(D, dtype=jnp.int32)
    inner_frac = (place_index % FEAT_COL).astype(jnp.float32) / FEAT_COL
    outer_frac = (place_index // FEAT_COL).astype(jnp.float32) / max(D // FEAT_COL - 1, 1)
    return jnp.sqrt((1.0 + growth * inner_frac) * (1.0 + growth * outer_frac))


def draw_segment_ids(key, part):
    key = jax.random.fold_in(key, 13)
    margin = SEQ_LEN // 8
    span_free = SEQ_LEN - 2 * margin - 1
    cut_count = DOCS - 1
    drawn = jax.random.randint(key, (SEQS, cut_count), 0, span_free)
    squared = drawn * drawn // span_free
    toward_start = jnp.arange(cut_count) % 2 == 0
    cut_place = jnp.where(toward_start[None, :], 1 + squared, span_free - squared)
    low_edge = SEQ_LEN // 2 - margin
    cut_place = jnp.where(cut_place >= low_edge, cut_place + 2 * margin, cut_place)
    place_index = jnp.arange(SEQ_LEN, dtype=jnp.int32)
    doc_ids = jnp.sum((cut_place[:, :, None] <= place_index[None, None, :]).astype(jnp.int32), axis=1)
    return doc_ids.astype(jnp.int32)


def draw_norm_gains(key, part):
    key = jax.random.fold_in(key, 11)
    jitter = 1.0 + 0.08 * jnp.clip(jax.random.normal(key, (2, D), jnp.float32), -3.0, 3.0)
    return 0.6 * rising(2.0)[None, :] * jitter


def draw_cotangent(key, part):
    key = jax.random.fold_in(key, 12)
    base_draw = jnp.clip(jax.random.normal(key, (TOKENS, D), jnp.float32), -4.0, 4.0)
    return (base_draw * (rising(2.0) / 2.0)[None, :]).astype(jnp.bfloat16)


def level_of(own_key, shape, pieces, least, high):
    gain, own = 1.0, jax.random.fold_in(own_key, 6)
    for dim, shards_of in pieces:
        steps = jnp.exp(jax.random.uniform(jax.random.fold_in(own, dim), (shards_of,), jnp.float32, least / len(pieces), high / len(pieces)))
        gain = gain * jnp.repeat(steps, shape[dim] // shards_of).reshape([-1 if axis == dim else 1 for axis in range(len(shape))])
    return gain


def scatter_about(key, dims, spread, limit, cuts=(), kind=jnp.bfloat16):
    values = spread * jax.random.normal(key, dims, jnp.float32)
    if cuts:
        values = values * level_of(key, dims, cuts, -0.22, 0.18)
    return jnp.clip(values, -limit, limit).astype(kind)


def setup_inputs(seed: int = 0) -> dict:
    seeds = jax.random.split(jax.random.key(seed), 23)
    tokens = scatter_about(seeds[0], (TOKENS, D), 1.0, 6.0, ((0, 8), (1, 4)))
    segment_ids = draw_segment_ids(jax.random.fold_in(seeds[22], 71), 0)
    cotangent = draw_cotangent(jax.random.fold_in(seeds[22], 71), 0)
    qkv_weight = scatter_about(seeds[3], (D, 3, H, HD), D ** -0.5, 0.1875, ((0, 4), (2, 2)))
    attn_weight = scatter_about(seeds[4], (H, HD, D), (H * HD // 32) ** -0.5, 1.0, ((0, 2), (2, 4)))
    in_weight = scatter_about(seeds[5], (D, 2, FF), D ** -0.5, 0.1875, ((0, 4), (2, 2)))
    out_weight = scatter_about(seeds[6], (FF, D), FF ** -0.5, 0.125, ((0, 2), (1, 4)))
    norm_gains = draw_norm_gains(jax.random.fold_in(seeds[22], 71), 0)
    qkv_master = scatter_about(seeds[8], (D, 3, H, HD), D ** -0.5, 0.1875, ((0, 16), (2, 2)), jnp.float32)
    attn_master = scatter_about(seeds[9], (H, HD, D), (H * HD) ** -0.5, 0.1875, ((0, 2), (2, 16)), jnp.float32)
    in_master = scatter_about(seeds[10], (D, 2, FF), D ** -0.5, 0.1875, ((0, 16), (2, 2)), jnp.float32)
    out_master = scatter_about(seeds[11], (FF, D), FF ** -0.5, 0.125, ((0, 2), (1, 16)), jnp.float32)
    qkv_first = scatter_about(seeds[12], (D, 3, H, HD), (0.11 * PARAMS ** -0.5), 0.00048828125, ((0, 16), (2, 2)), jnp.float32)
    attn_first = scatter_about(seeds[13], (H, HD, D), (0.11 * PARAMS ** -0.5), 0.00048828125, ((0, 2), (2, 16)), jnp.float32)
    in_first = scatter_about(seeds[14], (D, 2, FF), (0.11 * PARAMS ** -0.5), 0.00048828125, ((0, 16), (2, 2)), jnp.float32)
    out_first = scatter_about(seeds[15], (FF, D), (0.11 * PARAMS ** -0.5), 0.00048828125, ((0, 2), (1, 16)), jnp.float32)
    qkv_second = jnp.clip(jnp.exp(math.log(1.3053466751955511e-08) - 2.7725887 * jax.random.uniform(seeds[16], (D, 3, H, HD), jnp.float32) ** level_of(seeds[16], (D, 3, H, HD), ((0, 16), (2, 2)), -0.2, 0.2)), 8.158416719972195e-10, 1.3053466751955511e-08)
    attn_second = jnp.clip(jnp.exp(math.log(3.263366687988878e-09) - 2.3025851 * jax.random.uniform(seeds[17], (H, HD, D), jnp.float32) ** level_of(seeds[17], (H, HD, D), ((0, 2), (2, 16)), -0.2, 0.2)), 3.2633667990111803e-10, 3.263366687988878e-09)
    in_second = jnp.clip(jnp.exp(math.log(1.3053466751955511e-08) - 2.7725887 * jax.random.uniform(seeds[18], (D, 2, FF), jnp.float32) ** level_of(seeds[18], (D, 2, FF), ((0, 16), (2, 2)), -0.2, 0.2)), 8.158416719972195e-10, 1.3053466751955511e-08)
    out_second = jnp.clip(jnp.exp(math.log(1.3053466751955511e-08) - 2.7725887 * jax.random.uniform(seeds[19], (FF, D), jnp.float32) ** level_of(seeds[19], (FF, D), ((0, 2), (1, 16)), -0.2, 0.2)), 8.158416719972195e-10, 1.3053466751955511e-08)
    gains_first = scatter_about(seeds[20], (2, D), (0.11 * PARAMS ** -0.5), 0.00048828125, ((1, 4),), jnp.float32)
    gains_second = jnp.clip(jnp.exp(math.log(1.3053466751955511e-08) - 2.7725887 * jax.random.uniform(seeds[21], (2, D), jnp.float32) ** level_of(seeds[21], (2, D), ((1, 4),), -0.2, 0.2)), 8.158416719972195e-10, 1.3053466751955511e-08)
    return dict(tokens=tokens, segment_ids=segment_ids, cotangent=cotangent, qkv_weight=qkv_weight, attn_weight=attn_weight, in_weight=in_weight, out_weight=out_weight, norm_gains=norm_gains, qkv_master=qkv_master, attn_master=attn_master, in_master=in_master, out_master=out_master, qkv_first=qkv_first, attn_first=attn_first, in_first=in_first, out_first=out_first, qkv_second=qkv_second, attn_second=attn_second, in_second=in_second, out_second=out_second, gains_first=gains_first, gains_second=gains_second)


NORM_EPSILON = 1e-05
ROPE_BASE = 160000.0
CLIP_NORM = 1.0
LEARN_RATE = 0.02
GAIN_RATE = 0.5
BETA_ONE = 0.9
BETA_TWO = 0.98
ADAM_EPSILON = 1e-08
WEIGHT_DECAY = 0.01
MASKED = -1e+30
PRECISE = lax.Precision.HIGHEST

@jax.custom_vjp
def low(v):
    return lax.optimization_barrier(v.astype(jnp.bfloat16)).astype(jnp.float32)

@jax.custom_vjp
def low_back(v):
    return v

def low_keep(v):
    return (low(v), None)

def low_pass(kept, grad):
    return (grad,)

def back_keep(v):
    return (v, None)

def back_low(kept, grad):
    return (low(grad),)
low.defvjp(low_keep, low_pass)
low_back.defvjp(back_keep, back_low)

def norm_rows(values, gain_row):
    average = lax.optimization_barrier(jnp.mean(values, axis=-1, keepdims=True))
    centered = values - average
    variance = lax.optimization_barrier(jnp.mean(centered * centered, axis=-1, keepdims=True))
    return centered * lax.rsqrt(variance + NORM_EPSILON) * gain_row

def positions(segment):
    length = segment.shape[0]
    number = jnp.arange(length, dtype=jnp.int32)
    before = jnp.concatenate([segment[:1] - 1, segment[:-1]])
    change_marks = jnp.where(segment != before, number, jnp.zeros_like(number))
    return number - lax.cummax(change_marks, axis=0)

def angles(place_index, head_size):
    freq_index = jnp.arange(0, head_size, 2).astype(jnp.float32)
    frequency = ROPE_BASE ** (-freq_index / head_size)
    turned = place_index.astype(jnp.float32)[:, None] * frequency[None, :]
    turned = jnp.concatenate([turned, turned], axis=-1)
    return (jnp.cos(turned), jnp.sin(turned))

def rotate(values, cos_table, sin_table):
    half_size = values.shape[-1] // 2
    turned = jnp.concatenate([-values[..., half_size:], values[..., :half_size]], axis=-1)
    return values * cos_table[:, None, :] + turned * sin_table[:, None, :]

def attend(query_rows, key_rows, value_rows, segment):
    length = query_rows.shape[0]
    span_rows = min(512, length)
    scaling = HD ** (-0.5)
    query_blocks = query_rows.reshape(length // span_rows, span_rows, H, HD)
    segment_blocks = segment.reshape(length // span_rows, span_rows)

    def one_block(operands):
        query_part, segment_part = operands
        raw_scores = jnp.einsum('qhe,khe->hqk', query_part, key_rows, precision=PRECISE)
        scores = low_back(raw_scores * scaling)
        same_doc = segment_part[:, None] == segment[None, :]
        scores = jnp.where(same_doc[None, :, :], scores, MASKED)
        weights_low = low(jax.nn.softmax(scores, axis=-1))
        return jnp.einsum('hqk,khe->qhe', weights_low, value_rows, precision=PRECISE)
    mixed_heads = lax.map(jax.checkpoint(one_block), (query_blocks, segment_blocks))
    return mixed_heads.reshape(length, H, HD)

def forward_layer(params, inputs, segment):
    qkv_weight, attn_weight, in_weight, out_weight, gains = params
    cos_table, sin_table = angles(positions(segment), HD)
    first_norm = low(norm_rows(inputs, gains[0]))
    projected = low_back(jnp.einsum('td,dgne->tgne', first_norm, qkv_weight, precision=PRECISE))
    query_rows = low(rotate(projected[:, 0], cos_table, sin_table))
    key_rows = low(rotate(projected[:, 1], cos_table, sin_table))
    value_rows = low(projected[:, 2])
    mixed_heads = low(low_back(attend(query_rows, key_rows, value_rows, segment)))
    attn_part = low_back(jnp.einsum('the,hed->td', mixed_heads, attn_weight, precision=PRECISE))
    middle = inputs + attn_part
    second_norm = low(norm_rows(middle, gains[1]))
    up_gate = low_back(jnp.einsum('td,dgf->tgf', second_norm, in_weight, precision=PRECISE))
    hidden = low(jax.nn.gelu(up_gate[:, 0], approximate=False) * up_gate[:, 1])
    ffn_part = low_back(jnp.dot(hidden, out_weight, precision=PRECISE))
    return middle + ffn_part

def adam_update(master, first_moment, second, gradient, factor, decay_rate, step_rate):
    scaled = gradient * factor
    first_new = BETA_ONE * first_moment + (1.0 - BETA_ONE) * scaled
    second_new = BETA_TWO * second + (1.0 - BETA_TWO) * scaled * scaled
    first_hat = first_new / (1.0 - BETA_ONE ** STEP)
    second_hat = second_new / (1.0 - BETA_TWO ** STEP)
    master_new = master - step_rate * (first_hat / (jnp.sqrt(second_hat) + ADAM_EPSILON) + decay_rate * master)
    return (first_new, second_new, master_new)

def reference(tokens, segment_ids, cotangent, qkv_weight, attn_weight, in_weight, out_weight, norm_gains, qkv_master, attn_master, in_master, out_master, qkv_first, attn_first, in_first, out_first, qkv_second, attn_second, in_second, out_second, gains_first, gains_second):
    params = (qkv_weight.astype(jnp.float32), attn_weight.astype(jnp.float32), in_weight.astype(jnp.float32), out_weight.astype(jnp.float32), norm_gains)
    inputs = tokens.astype(jnp.float32).reshape(SEQS, SEQ_LEN, D)
    cot_rows = cotangent.astype(jnp.float32).reshape(SEQS, SEQ_LEN, D)

    def one_sequence(summed, operands):
        sequence, cot_part, segment = operands
        output, pullback = jax.vjp(lambda weights, values: forward_layer(weights, values, segment), params, sequence)
        gradients, input_part = pullback(cot_part)
        summed = jax.tree.map(jnp.add, summed, gradients)
        return (summed, (output.astype(jnp.bfloat16), input_part))
    zero_grads = jax.tree.map(jnp.zeros_like, params)
    summed, (outputs, input_parts) = lax.scan(one_sequence, zero_grads, (inputs, cot_rows, segment_ids))
    squares = sum((jnp.sum(member * member) for member in summed))
    grad_norm = jnp.sqrt(squares)
    factor = CLIP_NORM / (grad_norm + 1e-06)
    qkv_new = adam_update(qkv_master, qkv_first, qkv_second, summed[0], factor, WEIGHT_DECAY, LEARN_RATE)
    attn_new = adam_update(attn_master, attn_first, attn_second, summed[1], factor, WEIGHT_DECAY, LEARN_RATE)
    in_new = adam_update(in_master, in_first, in_second, summed[2], factor, WEIGHT_DECAY, LEARN_RATE)
    out_new = adam_update(out_master, out_first, out_second, summed[3], factor, WEIGHT_DECAY, LEARN_RATE)
    gains_new = adam_update(norm_gains, gains_first, gains_second, summed[4], factor, 0.0, GAIN_RATE)
    return (outputs.reshape(TOKENS, D), input_parts.reshape(TOKENS, D), grad_norm, qkv_new[0], attn_new[0], in_new[0], out_new[0], qkv_new[1], attn_new[1], in_new[1], out_new[1], qkv_new[2], attn_new[2], in_new[2], out_new[2], qkv_new[2].astype(jnp.bfloat16), attn_new[2].astype(jnp.bfloat16), in_new[2].astype(jnp.bfloat16), out_new[2].astype(jnp.bfloat16), gains_new[0], gains_new[1], gains_new[2])
```

```python
import functools
import math

import jax
import jax.numpy as jnp
from jax import lax
from jax.experimental import pallas as pl
from jax.experimental.pallas import tpu as pltpu
from jax.sharding import PartitionSpec as P

STEP = 10


NORM_EPSILON = 1e-05
ROPE_BASE = 160000.0
CLIP_NORM = 1.0
LEARN_RATE = 0.02
GAIN_RATE = 0.5
BETA_ONE = 0.9
BETA_TWO = 0.98
ADAM_EPSILON = 1e-08
WEIGHT_DECAY = 0.01
MASKED = -1e30

BLOCK = 256
LANES = 128
FF_PAD = 128
F32 = jnp.float32
BF16 = jnp.bfloat16

NT = (((1,), (1,)), ((), ()))
NN = (((1,), (0,)), ((), ()))
TN = (((0,), (0,)), ((), ()))


def mm(a, b, dims):
    return lax.dot_general(a, b, dims, preferred_element_type=F32)


VMEM = pl.BlockSpec(memory_space=pltpu.VMEM)
SMEM = pl.BlockSpec(memory_space=pltpu.SMEM)
PARAMS = pltpu.CompilerParams(vmem_limit_bytes=56 * 1024 * 1024)


def whole_call(body, outs, args, scratch=(), scalars=1, flops=0):
    moved = sum(a.size * a.dtype.itemsize for a in args) + sum(
        math.prod(s) * jnp.dtype(t).itemsize for s, t in outs
    )
    return pl.pallas_call(
        body,
        out_shape=[jax.ShapeDtypeStruct(s, t) for s, t in outs],
        in_specs=[SMEM] * scalars + [VMEM] * (len(args) - scalars),
        out_specs=[VMEM] * len(outs),
        scratch_shapes=list(scratch),
        compiler_params=PARAMS,
        cost_estimate=pl.CostEstimate(flops=flops, bytes_accessed=moved, transcendentals=0),
    )(*args)


def to_col(v, k):
    return lax.ppermute(v, "col", [(i, i ^ k) for i in range(4)])


def to_row(v):
    return lax.ppermute(v, "row", [(0, 1), (1, 0)])


def gather_col(v):
    half = v.shape[0] // 2
    a = to_col(v, 1)
    b = to_col(v, 2)
    d = jnp.concatenate([to_col(a[:half], 2), to_col(b[half:], 1)], axis=0)
    return [v, a, b, d]


def exchange_col(parts):
    return [parts[0]] + [to_col(parts[k], k) for k in range(1, 4)]


def sum_dp(v):
    n = lax.axis_size("dp")
    if n == 4:
        return v + sum(
            lax.ppermute(v, "dp", [(i, i ^ k) for i in range(4)]) for k in (1, 2, 3)
        )
    return lax.psum(v, "dp")


def scatter_dp(v):
    n = lax.axis_size("dp")
    if n != 4:
        return lax.psum_scatter(v, "dp", scatter_dimension=1, tiled=True).astype(F32)
    here = lax.axis_index("dp")
    rows = v.shape[1] // n
    split = v.reshape(v.shape[0], n, rows, v.shape[2])

    def piece(k):
        return lax.dynamic_index_in_dim(split, here ^ k, 1, keepdims=False)

    total = piece(0).astype(F32)
    for k in (1, 2, 3):
        total = total + lax.ppermute(piece(k), "dp", [(i, i ^ k) for i in range(4)]).astype(F32)
    return total


def natural(parts, here):
    stacked = jnp.stack(parts)
    return [lax.dynamic_index_in_dim(stacked, here ^ j, 0, keepdims=False) for j in range(4)]


def half_mask(shape):
    return lax.broadcasted_iota(jnp.int32, shape, len(shape) - 1) % LANES < 64


def swap_halves(v):
    lane = lax.broadcasted_iota(jnp.int32, v.shape, 1) % 64
    return jnp.where(lane < 32, pltpu.roll(v, LANES - 32, 1), pltpu.roll(v, 32, 1))


def moments(parts, features):
    average = sum(jnp.sum(v, axis=1, keepdims=True) for v in parts) / features
    centered = [v - average for v in parts]
    variance = sum(jnp.sum(v * v, axis=1, keepdims=True) for v in centered) / features
    inverse = lax.rsqrt(variance + NORM_EPSILON)
    return [v * inverse for v in centered], inverse


def lanes_of(ref, rows, p):
    return ref[rows, pl.ds(p * 256, 256)]


def qkv_kernel(x0, x1, x2, x3, gains, w_own, w_oth, cos, sin, own_out, oth_out, h_out):
    parts = [ref[...].astype(F32) for ref in (x0, x1, x2, x3)]
    units, _ = moments(parts, 4 * 256)
    low = [(units[k] * gains[k, 0:1, :]).astype(BF16) for k in range(4)]
    for k in range(4):
        h_out[:, k * 256 : (k + 1) * 256] = low[k]
    cos_part, sin_part = cos[...], sin[...]
    weight = [jnp.concatenate([w_own[k], w_oth[k]], axis=0) for k in range(4)]
    both = sum(mm(low[k], weight[k], NT) for k in range(4))
    for side, out in enumerate((own_out, oth_out)):
        got = both[:, side * 384 : (side + 1) * 384]
        query, key, value = got[:, :128], got[:, 128:256], got[:, 256:]
        query = (query * cos_part + swap_halves(query) * sin_part).astype(BF16)
        out[:, :128] = query * jnp.asarray(0.125, BF16)
        out[:, 128:256] = (key * cos_part + swap_halves(key) * sin_part).astype(BF16)
        out[:, 256:] = value.astype(BF16)


def run_qkv(xs, gains, w_own, w_oth, cos, sin):
    rows = xs[0].shape[0]
    step = 256
    whole = lambda shape: pl.BlockSpec(shape, lambda i: (0,) * len(shape))
    block = lambda n: pl.BlockSpec((step, n), lambda i: (i, 0))
    return pl.pallas_call(
        qkv_kernel,
        grid=(rows // step,),
        in_specs=[block(256)] * 4
        + [whole(gains.shape), whole(w_own.shape), whole(w_oth.shape), block(128), block(128)],
        out_specs=[block(384), block(384), block(1024)],
        out_shape=[
            jax.ShapeDtypeStruct((rows, 384), BF16),
            jax.ShapeDtypeStruct((rows, 384), BF16),
            jax.ShapeDtypeStruct((rows, 1024), BF16),
        ],
        compiler_params=PARAMS,
        cost_estimate=pl.CostEstimate(
            flops=2 * rows * 1024 * 768, bytes_accessed=8 * 1024 * 1024, transcendentals=0
        ),
    )(*xs, gains, w_own, w_oth, cos, sin)


def to_columns(row):
    return jnp.transpose(jnp.broadcast_to(row, (LANES, row.shape[1])))


def attend_kernel(info, own, recv, seg, own_out, oth_out, lse_out, qkv, score, mixed):
    length = qkv.shape[0]
    rows = length // 2
    here = info[4, 0]
    qkv[pl.ds(pl.multiple_of(here * rows, rows), rows), :] = own[...]
    qkv[pl.ds(pl.multiple_of((1 - here) * rows, rows), rows), :] = recv[...]
    low_half = half_mask((BLOCK, LANES))
    zero = jnp.zeros((BLOCK, LANES), BF16)

    def one_block(qb, _):
        at = pl.multiple_of(qb * BLOCK, BLOCK)
        query = qkv[pl.ds(at, BLOCK), :128]
        pair = jnp.concatenate(
            [jnp.where(low_half, query, zero), jnp.where(low_half, zero, query)], axis=0
        )
        low_block, high_block = info[0, qb], info[1, qb]
        q_first, q_last = info[2, qb], info[3, qb]

        def scores(kb, highest):
            k_at = pl.multiple_of(kb * BLOCK, BLOCK)
            key = qkv[pl.ds(k_at, BLOCK), 128:256]
            got = mm(pair, key, NT)
            inside = (info[2, kb] == q_last) & (info[3, kb] == q_first)

            @pl.when(inside)
            def _():
                score[:, pl.ds(k_at, BLOCK)] = got

            @pl.when(jnp.logical_not(inside))
            def _():
                seg_q = to_columns(seg[:, pl.ds(at, BLOCK)])
                seg_k = seg[:, pl.ds(k_at, BLOCK)]
                same = jnp.concatenate([seg_q, seg_q], axis=1) == seg_k
                score[:, pl.ds(k_at, BLOCK)] = jnp.where(
                    jnp.concatenate([same, same], axis=0), got, MASKED
                )

            got = score[:, pl.ds(k_at, BLOCK)]
            return jnp.maximum(highest, jnp.maximum(got[:, :128], got[:, 128:]))

        highest = lax.fori_loop(
            low_block, high_block, scores, jnp.full((2 * BLOCK, LANES), MASKED, F32)
        )
        highest = jnp.broadcast_to(jnp.max(highest, axis=1, keepdims=True), (2 * BLOCK, LANES))
        wide = jnp.concatenate([highest, highest], axis=1)

        def values(kb, carry):
            total, mixing = carry
            k_at = pl.multiple_of(kb * BLOCK, BLOCK)
            value = qkv[pl.ds(k_at, BLOCK), 256:]
            weight = jnp.exp(score[:, pl.ds(k_at, BLOCK)] - wide)
            total = total + weight[:, :128] + weight[:, 128:]
            return total, mixing + mm(weight.astype(BF16), value, NN)

        zeros = jnp.zeros((2 * BLOCK, LANES), F32)
        total, mixing = lax.fori_loop(low_block, high_block, values, (zeros, zeros))
        total = jnp.broadcast_to(jnp.sum(total, axis=1, keepdims=True), (2 * BLOCK, LANES))
        mixing = mixing / total
        lse = highest + jnp.log(total)
        mixed[pl.ds(at, BLOCK), :] = jnp.where(low_half, mixing[:BLOCK], mixing[BLOCK:]).astype(
            BF16
        )
        lse_t = jnp.transpose(jnp.where(low_half, lse[:BLOCK], lse[BLOCK:]))
        lse_out[0:1, pl.ds(at, BLOCK)] = lse_t[0:1, :]
        lse_out[1:2, pl.ds(at, BLOCK)] = lse_t[64:65, :]
        return 0

    lax.fori_loop(0, length // BLOCK, one_block, 0)
    own_out[...] = mixed[pl.ds(pl.multiple_of(here * rows, rows), rows), :]
    oth_out[...] = mixed[pl.ds(pl.multiple_of((1 - here) * rows, rows), rows), :]


def attend_back_kernel(
    info, own, recv, seg, lse, mix_own, mix_oth, dm_own, dm_recv, cos, sin,
    own_out, oth_out, qkv, dmix, dsum, dquery, dout,
):
    length = qkv.shape[0]
    rows = length // 2
    here = info[4, 0]
    mine = pl.ds(pl.multiple_of(here * rows, rows), rows)
    other = pl.ds(pl.multiple_of((1 - here) * rows, rows), rows)
    qkv[mine, :] = own[...]
    qkv[other, :] = recv[...]
    dmix[mine, :] = dm_own[...]
    dmix[other, :] = dm_recv[...]
    dquery[mine, :] = mix_own[...].astype(F32)
    dquery[other, :] = mix_oth[...].astype(F32)
    blocks = length // BLOCK

    def inner(qb, _):
        at = pl.multiple_of(qb * BLOCK, BLOCK)
        product = jnp.transpose(dmix[pl.ds(at, BLOCK), :].astype(F32) * dquery[pl.ds(at, BLOCK), :])
        dsum[0:1, pl.ds(at, BLOCK)] = jnp.sum(product[:64], axis=0, keepdims=True)
        dsum[1:2, pl.ds(at, BLOCK)] = jnp.sum(product[64:], axis=0, keepdims=True)
        dquery[pl.ds(at, BLOCK), :] = jnp.zeros((BLOCK, LANES), F32)
        return 0

    lax.fori_loop(0, blocks, inner, 0)
    low_half = half_mask((BLOCK, LANES))
    zero = jnp.zeros((BLOCK, LANES), BF16)

    def both(v):
        return jnp.concatenate([jnp.where(low_half, v, zero), jnp.where(low_half, zero, v)], axis=0)

    def one_block(kb, _):
        k_at = pl.multiple_of(kb * BLOCK, BLOCK)
        key_pair = both(qkv[pl.ds(k_at, BLOCK), 128:256])
        value_pair = both(qkv[pl.ds(k_at, BLOCK), 256:])
        k_first, k_last = info[2, kb], info[3, kb]
        seg_k = to_columns(seg[:, pl.ds(k_at, BLOCK)])
        seg_k = jnp.concatenate([seg_k, seg_k], axis=1)
        zeros = jnp.zeros((2 * BLOCK, LANES), F32)

        def rows_of(ref, at):
            return jnp.concatenate(
                [
                    jnp.broadcast_to(ref[0:1, pl.ds(at, BLOCK)], (BLOCK, BLOCK)),
                    jnp.broadcast_to(ref[1:2, pl.ds(at, BLOCK)], (BLOCK, BLOCK)),
                ],
                axis=0,
            )

        def step(qb, carry):
            dkey, dvalue = carry
            at = pl.multiple_of(qb * BLOCK, BLOCK)
            query = qkv[pl.ds(at, BLOCK), :128]
            grad = dmix[pl.ds(at, BLOCK), :]
            got = mm(key_pair, query, NT) - rows_of(lse, at)
            inside = (info[2, qb] == k_last) & (info[3, qb] == k_first)
            same = seg_k == seg[:, pl.ds(at, BLOCK)]
            same = jnp.logical_or(jnp.concatenate([same, same], axis=0), inside)
            weight = jnp.where(same, jnp.exp(got), 0.0)
            dweight = mm(value_pair, grad, NT)
            dscore = (weight * (dweight - rows_of(dsum, at))).astype(BF16)
            dvalue = dvalue + mm(weight.astype(BF16), grad, NN)
            dkey = dkey + mm(dscore, query, NN)
            dquery[pl.ds(at, BLOCK), :] += mm(dscore, key_pair, TN)
            return dkey, dvalue

        dkey, dvalue = lax.fori_loop(info[0, kb], info[1, kb], step, (zeros, zeros))
        dkey = jnp.where(low_half, dkey[:BLOCK], dkey[BLOCK:])
        dvalue = jnp.where(low_half, dvalue[:BLOCK], dvalue[BLOCK:])
        cos_part, sin_part = cos[pl.ds(k_at, BLOCK), :], sin[pl.ds(k_at, BLOCK), :]
        dkey = dkey * cos_part - swap_halves(dkey) * sin_part
        dout[pl.ds(k_at, BLOCK), 128:256] = dkey.astype(BF16)
        dout[pl.ds(k_at, BLOCK), 256:] = dvalue.astype(BF16)
        return 0

    lax.fori_loop(0, blocks, one_block, 0)

    def finish(qb, _):
        at = pl.multiple_of(qb * BLOCK, BLOCK)
        cos_part, sin_part = cos[pl.ds(at, BLOCK), :], sin[pl.ds(at, BLOCK), :]
        grad = dquery[pl.ds(at, BLOCK), :] * 0.125
        grad = grad * cos_part - swap_halves(grad) * sin_part
        dout[pl.ds(at, BLOCK), :128] = grad.astype(BF16)
        return 0

    lax.fori_loop(0, blocks, finish, 0)
    own_out[...] = dout[mine, :]
    oth_out[...] = dout[other, :]


def slot_rows(info, k):
    return pl.ds(pl.multiple_of((info[4, 1] ^ k) * 256, 256), 256)


def attn_out_kernel(info, mix_own, mix_oth, w_own, w_oth, *outs):
    for k in range(4):
        rows = slot_rows(info, k)
        mix = jnp.concatenate([mix_own[rows, :], mix_oth[rows, :]], axis=1)
        for p in range(4):
            weight = jnp.concatenate([w_own[k ^ p, :128], w_oth[k ^ p, :128]], axis=0)
            outs[k][:, p * 256 : (p + 1) * 256] = mm(mix, weight, NN).astype(BF16)


def middle_kernel(info, x0, x1, x2, x3, p0, p1, p2, p3, out):
    rows = slot_rows(info, 0)
    for p, x in enumerate((x0, x1, x2, x3)):
        at = slice(p * 256, (p + 1) * 256)
        total = x[rows, :].astype(F32)
        for part in (p0, p1, p2, p3):
            total = total + part[:, at].astype(F32)
        out[:, at] = total.astype(BF16)


def ffn_kernel(
    index, m0, m1, m2, m3, d0, d1, d2, d3, gains, w_own, w_oth,
    f0, f1, f2, f3, g0, g1, g2, g3, h_out, hid_out, dug_out, mid_out, mid,
):
    slot = pl.program_id(0)
    for k, part in enumerate((m0, m1, m2, m3)):

        @pl.when(slot == k)
        def _(k=k, part=part):
            for p in range(4):
                mid[:, p * 256 : (p + 1) * 256] = part[:, (k ^ p) * 256 : ((k ^ p) + 1) * 256]

    parts = [mid[:, p * 256 : (p + 1) * 256].astype(F32) for p in range(4)]
    mid_out[...] = mid[:, :256]
    units, _ = moments(parts, 4 * 256)
    low = [(units[p] * gains[p, 1:2, :]).astype(BF16) for p in range(4)]
    for p in range(4):
        h_out[:, p * 256 : (p + 1) * 256] = low[p]
    grads = [ref[...] for ref in (d0, d1, d2, d3)]

    def weight(p, first):
        return jnp.concatenate(
            [w_own[p, first : first + 384], w_oth[p, first : first + 384]], axis=0
        )

    gate = sum(mm(low[p], weight(p, 128), NT) for p in range(4))
    up = sum(mm(low[p], weight(p, 512), NT) for p in range(4))
    dhidden = sum(mm(grads[p], weight(p, 896), NT) for p in range(4))
    phi = 0.5 * (1.0 + lax.erf(gate * (2.0**-0.5)))
    density = jnp.exp(-0.5 * gate * gate) * ((2.0 * math.pi) ** -0.5)
    act = gate * phi
    hidden = (act * up).astype(BF16)
    dgate = (dhidden * up * (phi + gate * density)).astype(BF16)
    dup = (dhidden * act).astype(BF16)
    hid_out[...] = hidden
    dug_out[:, :384] = dgate[:, :384]
    dug_out[:, 384:768] = dup[:, :384]
    dug_out[:, 768:1152] = dgate[:, 384:]
    dug_out[:, 1152:] = dup[:, 384:]
    for p, out in enumerate((f0, f1, f2, f3)):
        out[...] = mm(hidden, weight(p, 896), NN).astype(BF16)
    back = [
        (mm(dgate, weight(p, 128), NN) + mm(dup, weight(p, 512), NN)).astype(BF16)
        for p in range(4)
    ]
    for k, out in enumerate((g0, g1, g2, g3)):

        @pl.when(slot == k)
        def _(k=k, out=out):
            for p in range(4):
                out[:, p * 256 : (p + 1) * 256] = back[k ^ p]


def run_ffn(index, mids, grads, gains, w_own, w_oth):
    rows = grads[0].shape[0]
    whole = lambda shape: pl.BlockSpec(shape, lambda i, s: (0,) * len(shape))
    block = lambda n: pl.BlockSpec((256, n), lambda i, s: (i ^ s[0], 0))
    shape = lambda r, n: jax.ShapeDtypeStruct((r, n), BF16)
    return pl.pallas_call(
        ffn_kernel,
        grid_spec=pltpu.PrefetchScalarGridSpec(
            num_scalar_prefetch=1,
            grid=(4,),
            in_specs=[whole((256, 1024))] * 4
            + [block(256)] * 4
            + [whole(gains.shape), whole(w_own.shape), whole(w_oth.shape)],
            out_specs=[block(256)] * 4
            + [whole((256, 1024))] * 4
            + [block(1024), block(768), block(1536), block(256)],
            scratch_shapes=[pltpu.VMEM((256, 1024), BF16)],
        ),
        out_shape=[shape(rows, 256)] * 4
        + [shape(256, 1024)] * 4
        + [shape(rows, 1024), shape(rows, 768), shape(rows, 1536), shape(rows, 256)],
        compiler_params=PARAMS,
        cost_estimate=pl.CostEstimate(
            flops=12 * rows * 1024 * 768, bytes_accessed=24 * 1024 * 1024, transcendentals=0
        ),
    )(index, *mids, *grads, gains, w_own, w_oth)


def norm_back(grads, units, inverse, gains):
    scaled = [g * w for g, w in zip(grads, gains)]
    first = sum(jnp.sum(v, axis=1, keepdims=True) for v in scaled) / 1024
    second = sum(jnp.sum(v * u, axis=1, keepdims=True) for v, u in zip(scaled, units)) / 1024
    return [inverse * (v - first - u * second) for v, u in zip(scaled, units)]


def middle_back_kernel(info, mid, p0, p1, p2, p3, d0, d1, d2, d3, gains, dx_out, dz_out, gain_out):
    rows = slot_rows(info, 0)
    at = [slice(p * 256, (p + 1) * 256) for p in range(4)]
    units, inverse = moments([mid[:, a].astype(F32) for a in at], 1024)
    grads = [sum(part[:, a].astype(F32) for part in (p0, p1, p2, p3)) for a in at]
    back = norm_back(grads, units, inverse, [gains[p, 1:2, :] for p in range(4)])
    for p, dy in enumerate((d0, d1, d2, d3)):
        total = back[p] + dy[rows, :].astype(F32)
        dx_out[:, at[p]] = total
        dz_out[:, at[p]] = total.astype(BF16)
        gain_out[p : p + 1, :] = jnp.sum(grads[p] * units[p], axis=0, keepdims=True)


def mixed_back_kernel(info, z0, z1, z2, z3, w_own, w_oth, own_out, oth_out, dz_out):
    for k, part in enumerate((z0, z1, z2, z3)):
        rows = slot_rows(info, k)
        total = None
        for p in range(4):
            piece = part[:, (k ^ p) * 256 : ((k ^ p) + 1) * 256]
            dz_out[rows, p * 256 : (p + 1) * 256] = piece
            weight = jnp.concatenate([w_own[p, :128], w_oth[p, :128]], axis=0)
            term = mm(piece, weight, NT)
            total = term if total is None else total + term
        own_out[rows, :] = total[:, :128].astype(BF16)
        oth_out[rows, :] = total[:, 128:].astype(BF16)


def input_back_kernel(info, d_own, d_oth, w_own, w_oth, h, gains, o0, o1, o2, o3, gain_out):
    sums = [None] * 4
    for k, out in enumerate((o0, o1, o2, o3)):
        rows = slot_rows(info, k)
        grad = jnp.concatenate([d_own[rows, :], d_oth[rows, :]], axis=1)
        for p in range(4):
            weight = jnp.concatenate([w_own[p], w_oth[p]], axis=0)
            got = mm(grad, weight, NN)
            out[:, (k ^ p) * 256 : ((k ^ p) + 1) * 256] = got.astype(BF16)
            part = jnp.sum(got * h[rows, p * 256 : (p + 1) * 256].astype(F32), axis=0, keepdims=True)
            sums[p] = part if sums[p] is None else sums[p] + part
    for p in range(4):
        gain_out[p : p + 1, :] = sums[p] / gains[p, 0:1, :]


def input_grad_kernel(info, x0, x1, x2, x3, p0, p1, p2, p3, dx, gains, o0, o1, o2, o3):
    rows = slot_rows(info, 0)
    at = [slice(p * 256, (p + 1) * 256) for p in range(4)]
    units, inverse = moments([x[rows, :].astype(F32) for x in (x0, x1, x2, x3)], 1024)
    grads = [sum(part[:, a].astype(F32) for part in (p0, p1, p2, p3)) for a in at]
    back = norm_back(grads, units, inverse, [gains[p, 0:1, :] for p in range(4)])
    for p, out in enumerate((o0, o1, o2, o3)):
        out[...] = (back[p] + dx[:, at[p]]).astype(BF16)


def adam_update(master, first_moment, second, gradient, factor, decay_rate, step_rate):
    scaled = gradient * factor
    first_new = BETA_ONE * first_moment + (1.0 - BETA_ONE) * scaled
    second_new = BETA_TWO * second + (1.0 - BETA_TWO) * scaled * scaled
    first_hat = first_new / (1.0 - BETA_ONE**STEP)
    second_hat = second_new / (1.0 - BETA_TWO**STEP)
    master_new = master - step_rate * (
        first_hat / (jnp.sqrt(second_hat) + ADAM_EPSILON) + decay_rate * master
    )
    return (first_new, second_new, master_new)


def positions(segment):
    length = segment.shape[0]
    number = jnp.arange(length, dtype=jnp.int32)
    before = jnp.concatenate([segment[:1] - 1, segment[:-1]])
    change_marks = jnp.where(segment != before, number, jnp.zeros_like(number))
    return number - lax.cummax(change_marks, axis=0)


def rope_tables(place):
    lane = jnp.arange(LANES) % 64
    frequency = ROPE_BASE ** (-(2.0 * (lane % 32).astype(F32)) / 64)
    turned = place.astype(F32)[:, None] * frequency[None, :]
    sign = jnp.where(lane < 32, -1.0, 1.0)
    return jnp.cos(turned), jnp.sin(turned) * sign[None, :]


def on_device(
    tokens, segment_ids, cotangent, qkv_weight, attn_weight, in_weight, out_weight, norm_gains,
    qkv_master, attn_master, in_master, out_master,
    qkv_first, attn_first, in_first, out_first,
    qkv_second, attn_second, in_second, out_second,
    gains_first, gains_second,
):
    col, row = lax.axis_index("col"), lax.axis_index("row")
    segment = segment_ids[0]
    length = segment.shape[0]
    rows = length // 2
    blocks = length // BLOCK
    ff_here = in_weight.shape[2] // 4
    ff_pad = -ff_here % FF_PAD
    ff_wide = ff_here + ff_pad

    qkv_t = jnp.transpose(qkv_weight, (1, 2, 3, 0))
    attn_t = attn_weight.reshape(4, LANES, 256)
    in_t = jnp.transpose(in_weight, (1, 2, 0)).reshape(2, 4, ff_here, 256)
    out_t = out_weight.reshape(4, ff_here, 256)

    def qkv_piece(k):
        return lax.dynamic_slice_in_dim(qkv_t, 2 * (col ^ k), 2, 1).reshape(3 * LANES, 256)

    def rest_piece(k):
        j = col ^ k
        inner = lax.dynamic_index_in_dim(in_t, j, 1, keepdims=False)
        return jnp.concatenate(
            [
                lax.dynamic_index_in_dim(attn_t, j, 0, keepdims=False),
                inner[0],
                inner[1],
                lax.dynamic_index_in_dim(out_t, j, 0, keepdims=False),
            ],
            axis=0,
        )

    xs = gather_col(tokens)
    gains = jnp.stack(exchange_col([norm_gains] * 4))
    wq_own = jnp.stack(exchange_col([qkv_piece(k) for k in range(4)]))
    wq_oth = to_row(wq_own)
    dys = gather_col(cotangent)
    rest = exchange_col([rest_piece(k) for k in range(4)])
    fill = jnp.zeros((ff_pad, 256), BF16)

    def padded(v):
        pieces = [v[:LANES]]
        for i in range(3):
            at = LANES + i * ff_here
            pieces += [v[at : at + ff_here], fill]
        return jnp.concatenate(pieces, axis=0)

    wr_own = jnp.stack([padded(v) for v in rest])
    wr_oth = to_row(wr_own)

    first = segment[::BLOCK]
    last = segment[BLOCK - 1 :: BLOCK]
    low = jnp.sum((segment[None, :] < first[:, None]).astype(jnp.int32), axis=1) // BLOCK
    high = (
        jnp.sum((segment[None, :] <= last[:, None]).astype(jnp.int32), axis=1) + BLOCK - 1
    ) // BLOCK
    place_here = jnp.zeros((blocks,), jnp.int32).at[0].set(row).at[1].set(col)
    info = jnp.stack([low, high, first, last, place_here])
    seg_row = segment_ids.astype(F32)
    cos, sin = rope_tables(positions(segment))
    cos_here = lax.dynamic_slice_in_dim(cos, row * rows, rows, 0)
    sin_here = lax.dynamic_slice_in_dim(sin, row * rows, rows, 0)

    own, oth, h1 = run_qkv(xs, gains, wq_own, wq_oth, cos_here, sin_here)
    recv = to_row(oth)
    h1_recv = to_row(h1)
    dense = 4 * length * length * LANES
    mix_own, mix_away, lse = whole_call(
        attend_kernel,
        [((rows, LANES), BF16), ((rows, LANES), BF16), ((2, length), F32)],
        (info, own, recv, seg_row),
        [
            pltpu.VMEM((length, 384), BF16),
            pltpu.VMEM((2 * BLOCK, length), F32),
            pltpu.VMEM((length, LANES), BF16),
        ],
        flops=4 * dense,
    )
    mix_oth = to_row(mix_away)
    parts = whole_call(
        attn_out_kernel,
        [((256, 1024), BF16)] * 4,
        (info, mix_own, mix_oth, wr_own, wr_oth),
        flops=2 * rows * 256 * 1024,
    )
    parts = exchange_col(parts)
    (middle,) = whole_call(middle_kernel, [((256, 1024), BF16)], (info, *xs, *parts))
    mids = gather_col(middle)
    index = jnp.reshape(col, (1,))
    ffn = run_ffn(index, mids, dys, gains, wr_own, wr_oth)
    forward, backward = ffn[:4], ffn[4:8]
    h2, hidden, dug, mid_here = ffn[8:]
    backward = exchange_col(backward)
    dx_mid, dz, gain_two = whole_call(
        middle_back_kernel,
        [((256, 1024), F32), ((256, 1024), BF16), ((4, 256), F32)],
        (info, middle, *backward, *dys, gains),
    )
    dzs = gather_col(dz)

    dy_all = jnp.concatenate(dys, axis=1)
    grad_in = mm(h2, dug, TN).astype(BF16)
    grad_out = mm(dy_all, hidden, TN).astype(BF16)
    ffn_own = jnp.concatenate([grad_in[:, : 2 * ff_wide], grad_out[:, :ff_wide]], axis=1)
    ffn_oth = jnp.concatenate([grad_in[:, 2 * ff_wide :], grad_out[:, ff_wide:]], axis=1)
    ffn_sum = (ffn_own.astype(F32) + to_row(ffn_oth).astype(F32)).astype(BF16)
    ffn_grad = lax.psum_scatter(
        ffn_sum.reshape(4, 256, 3 * ff_wide), "dp", scatter_dimension=1, tiled=True
    ).astype(F32)

    forward = exchange_col(forward)
    layer_out = (mid_here.astype(F32) + sum(v.astype(F32) for v in forward)).astype(BF16)

    dm_own, dm_away, dz_here = whole_call(
        mixed_back_kernel,
        [((rows, LANES), BF16), ((rows, LANES), BF16), ((rows, 1024), BF16)],
        (info, *dzs, wr_own, wr_oth),
        flops=2 * rows * 256 * 1024,
    )
    dm_recv = to_row(dm_away)
    dq_own, dq_away = whole_call(
        attend_back_kernel,
        [((rows, 384), BF16), ((rows, 384), BF16)],
        (info, own, recv, seg_row, lse, mix_own, mix_away, dm_own, dm_recv, cos, sin),
        [
            pltpu.VMEM((length, 384), BF16),
            pltpu.VMEM((length, LANES), BF16),
            pltpu.VMEM((2, length), F32),
            pltpu.VMEM((length, LANES), F32),
            pltpu.VMEM((length, 384), BF16),
        ],
        flops=10 * dense,
    )
    dq_oth = to_row(dq_away)

    attn_both = mm(dz_here, jnp.concatenate([mix_own, mix_oth], axis=1), TN)
    attn_sum = (attn_both[:, :LANES] + to_row(attn_both[:, LANES:].astype(BF16)).astype(F32)).astype(
        BF16
    )
    qkv_sum = (mm(h1, dq_own, TN) + mm(h1_recv, dq_away, TN)).astype(BF16)
    tail = jnp.concatenate([qkv_sum, attn_sum], axis=1).reshape(4, 256, 512)
    tail_grad = scatter_dp(tail)

    *partial_first, gain_one = whole_call(
        input_back_kernel,
        [((256, 1024), BF16)] * 4 + [((4, 256), F32)],
        (info, dq_own, dq_oth, wq_own, wq_oth, h1, gains),
        flops=2 * rows * 768 * 1024,
    )
    partial_first = exchange_col(partial_first)
    pieces = whole_call(
        input_grad_kernel,
        [((256, 256), BF16)] * 4,
        (info, *xs, *partial_first, dx_mid, gains),
    )
    input_grad = jnp.concatenate(natural(exchange_col(pieces), col), axis=0).astype(F32)

    gain_part = jnp.stack([gain_one, gain_two], axis=1)
    gain_grad = sum(exchange_col([gain_part[k] for k in range(4)]))
    gain_grad = sum_dp(gain_grad)
    gain_grad = gain_grad + to_row(gain_grad)
    lead_device = (lax.axis_index("dp") == 0) & (row == 0)
    total = (
        jnp.sum(ffn_grad * ffn_grad)
        + jnp.sum(tail_grad * tail_grad)
        + jnp.where(lead_device, jnp.sum(gain_grad * gain_grad), 0.0)
    )
    total = jnp.full((8, LANES), total)
    total = sum_dp(total)
    total = sum(exchange_col([total] * 4))
    total = total + to_row(total)
    grad_norm = jnp.sqrt(total[0, 0])
    factor = CLIP_NORM / (grad_norm + 1e-06)

    shard = tail_grad.shape[1]
    tail_low = tail_grad.astype(BF16)
    tail_nat = natural(exchange_col([tail_low[k] for k in range(4)]), col)
    grad_qkv = jnp.stack(
        [v[:, : 3 * LANES].reshape(shard, 3, 2, 64) for v in tail_nat], axis=2
    ).reshape(qkv_master.shape)
    grad_attn = jnp.concatenate([v[:, 3 * LANES :] for v in tail_nat], axis=1).T.reshape(
        attn_master.shape
    )
    ffn_low = ffn_grad.astype(BF16)
    ffn_nat = natural(exchange_col([ffn_low[k] for k in range(4)]), col)
    grad_in = jnp.stack(
        [
            jnp.concatenate([v[:, i * ff_wide : i * ff_wide + ff_here] for v in ffn_nat], axis=1)
            for i in range(2)
        ],
        axis=1,
    )
    grad_out = jnp.concatenate(
        [v[:, 2 * ff_wide : 2 * ff_wide + ff_here] for v in ffn_nat], axis=1
    ).T

    grad_qkv, grad_attn, grad_in, grad_out = (
        v.astype(F32) for v in (grad_qkv, grad_attn, grad_in, grad_out)
    )
    qkv_new = adam_update(
        qkv_master, qkv_first, qkv_second, grad_qkv, factor, WEIGHT_DECAY, LEARN_RATE
    )
    attn_new = adam_update(
        attn_master, attn_first, attn_second, grad_attn, factor, WEIGHT_DECAY, LEARN_RATE
    )
    in_new = adam_update(in_master, in_first, in_second, grad_in, factor, WEIGHT_DECAY, LEARN_RATE)
    out_new = adam_update(
        out_master, out_first, out_second, grad_out, factor, WEIGHT_DECAY, LEARN_RATE
    )
    gains_new = adam_update(
        norm_gains, gains_first, gains_second, gain_grad, factor, 0.0, GAIN_RATE
    )
    return (
        layer_out, input_grad, grad_norm,
        qkv_new[0], attn_new[0], in_new[0], out_new[0],
        qkv_new[1], attn_new[1], in_new[1], out_new[1],
        qkv_new[2], attn_new[2], in_new[2], out_new[2],
        qkv_new[2].astype(BF16), attn_new[2].astype(BF16),
        in_new[2].astype(BF16), out_new[2].astype(BF16),
        gains_new[0], gains_new[1], gains_new[2],
    )


def solution(mesh):
    activations = P(("dp", "row"), "col")
    gains = P(None, "col")
    weights = (
        P("col", None, "row", None), P("row", None, "col"), P("col", None, "row"), P("row", "col"),
    )
    states = (
        P(("col", "dp"), None, "row", None), P("row", None, ("col", "dp")),
        P(("col", "dp"), None, "row"), P("row", ("col", "dp")),
    )
    return jax.shard_map(
        on_device,
        mesh=mesh,
        in_specs=(activations, P("dp", None), activations, *weights, gains)
        + states * 3
        + (gains, gains),
        out_specs=(activations, activations, P()) + states * 4 + (gains, gains, gains),
        check_vma=False,
    )
```

```python
import functools
import math

import jax
import jax.numpy as jnp
from jax import lax
from jax.experimental import pallas as pl
from jax.experimental.pallas import tpu as pltpu
from jax.sharding import PartitionSpec as P

STEP = 10


NORM_EPSILON = 1e-05
ROPE_BASE = 160000.0
CLIP_NORM = 1.0
LEARN_RATE = 0.02
GAIN_RATE = 0.5
BETA_ONE = 0.9
BETA_TWO = 0.98
ADAM_EPSILON = 1e-08
WEIGHT_DECAY = 0.01
MASKED = -1e30
SIZES = (1, 2, 3, 4, 6, 8)

BLOCK = 256
LANES = 128
FF_PAD = 128
F32 = jnp.float32
BF16 = jnp.bfloat16

NT = (((1,), (1,)), ((), ()))
NN = (((1,), (0,)), ((), ()))
TN = (((0,), (0,)), ((), ()))


def mm(a, b, dims):
    return lax.dot_general(a, b, dims, preferred_element_type=F32)


VMEM = pl.BlockSpec(memory_space=pltpu.VMEM)
SMEM = pl.BlockSpec(memory_space=pltpu.SMEM)

def room(mib):
    return pltpu.CompilerParams(vmem_limit_bytes=mib * 1024 * 1024)


COST = pl.CostEstimate(flops=1024, bytes_accessed=1024, transcendentals=0)


def whole_call(body, outs, args, scratch=(), scalars=1, extra=6, away=0):
    inside = len(args) - scalars - away
    held = sum(
        math.prod(a.shape) * a.dtype.itemsize
        for a in (*args[: scalars + inside], *scratch)
        if a.dtype in (F32, BF16)
    ) + sum(math.prod(s) * jnp.dtype(t).itemsize for s, t in outs)
    return pl.pallas_call(
        body,
        out_shape=[jax.ShapeDtypeStruct(s, t) for s, t in outs],
        in_specs=[SMEM] * scalars
        + [VMEM] * inside
        + [pl.BlockSpec(memory_space=pltpu.HBM)] * away,
        out_specs=[VMEM] * len(outs),
        scratch_shapes=list(scratch),
        compiler_params=room(held // 2**20 + extra),
        cost_estimate=COST,
    )(*args)


def to_col(v, k):
    return lax.ppermute(v, "col", [(i, i ^ k) for i in range(4)])


def to_row(v):
    return lax.ppermute(v, "row", [(0, 1), (1, 0)])


def gather_col(v):
    half = v.shape[0] // 2
    a = to_col(v, 1)
    b = to_col(v, 2)
    d = jnp.concatenate([to_col(a[:half], 2), to_col(b[half:], 1)], axis=0)
    return [v, a, b, d]


def exchange_col(parts):
    return [parts[0]] + [to_col(parts[k], k) for k in range(1, 4)]


def after(values, *gates):
    tied = lax.optimization_barrier((values, gates))
    return tied[0]


def sum_dp(v):
    n = lax.axis_size("dp")
    if n == 4:
        return v + sum(
            lax.ppermute(v, "dp", [(i, i ^ k) for i in range(4)]) for k in (1, 2, 3)
        )
    return lax.psum(v, "dp")


def scatter_dp(v):
    if lax.axis_size("dp") != 4:
        return lax.psum_scatter(v, "dp", scatter_dimension=0).astype(F32)
    here = lax.axis_index("dp")
    piece = lambda k: lax.dynamic_index_in_dim(v, here ^ k, 0, keepdims=False)
    total = piece(0).astype(F32)
    for k in (1, 2, 3):
        total = total + lax.ppermute(piece(k), "dp", [(i, i ^ k) for i in range(4)]).astype(F32)
    return total


def natural(parts, here):
    stacked = jnp.stack(parts) if isinstance(parts, list) else parts
    return [lax.dynamic_index_in_dim(stacked, here ^ j, 0, keepdims=False) for j in range(4)]


def half_mask(shape):
    return lax.broadcasted_iota(jnp.int32, shape, len(shape) - 1) % LANES < 64


def swap_halves(v):
    lane = lax.broadcasted_iota(jnp.int32, v.shape, 1) % 64
    return jnp.where(lane < 32, pltpu.roll(v, LANES - 32, 1), pltpu.roll(v, 32, 1))


def rope_of(table):
    first = lax.broadcasted_iota(jnp.int32, table.shape, 1) % 64 < 32
    cos_part = jnp.where(first, table, pltpu.roll(table, 32, 1))
    sin_part = jnp.where(first, -pltpu.roll(table, LANES - 32, 1), table)
    return cos_part, sin_part


def moments(parts, features):
    average = sum(jnp.sum(v, axis=1, keepdims=True) for v in parts) / features
    centered = [v - average for v in parts]
    variance = sum(jnp.sum(v * v, axis=1, keepdims=True) for v in centered) / features
    inverse = lax.rsqrt(variance + NORM_EPSILON)
    return [v * inverse for v in centered], inverse


def lanes_of(ref, rows, p):
    return ref[rows, pl.ds(p * 256, 256)]


def project(low, w_own, table, out):
    cos_part, sin_part = rope_of(table[...])
    got = sum(mm(low[k], w_own[k, :384], NT) for k in range(4))
    query, key, value = got[:, :128], got[:, 128:256], got[:, 256:]
    query = (query * cos_part + swap_halves(query) * sin_part).astype(BF16)
    out[:, :128] = query * jnp.asarray(0.125, BF16)
    out[:, 128:256] = (key * cos_part + swap_halves(key) * sin_part).astype(BF16)
    out[:, 256:] = value.astype(BF16)


def qkv_kernel(
    index, x0, x1, x2, x3a, x3b, gains, w_own, table, own_out, h_out, inv_out, slot_out, x3
):
    step = pl.program_id(0)
    halves = pl.num_programs(0) // 2

    @pl.when(step < halves)
    def _():
        x3[...] = x3a[...]

    @pl.when(step >= halves)
    def _():
        x3[...] = x3b[...]

    refs = (x0, x1, x2, x3)

    @pl.when(step == index[0])
    def _():
        for k, ref in enumerate(refs):
            slot_out[:, k * 256 : (k + 1) * 256] = ref[...]

    parts = [ref[...].astype(F32) for ref in refs]
    units, inverse = moments(parts, 4 * 256)
    inv_out[...] = jnp.broadcast_to(inverse, inv_out.shape)
    low = [(units[k] * gains[k, 0:1, :]).astype(BF16) for k in range(4)]
    for k in range(4):
        h_out[:, k * 256 : (k + 1) * 256] = low[k]
    project(low, w_own, table, own_out)


def away_kernel(index, h, w_own, table, out):
    low = [h[:, k * 256 : (k + 1) * 256] for k in range(4)]
    project(low, w_own, table, out)


def run_qkv(index, xs, gains, w_own, table):
    rows = xs[0].shape[0]
    step = 256
    last = rows // step // 2 - 1
    whole = lambda shape: pl.BlockSpec(shape, lambda i, s: (0,) * len(shape))
    block = lambda n: pl.BlockSpec((step, n), lambda i, s: (i, 0))
    shape = lambda n, t=BF16: jax.ShapeDtypeStruct((rows, n), t)
    return pl.pallas_call(
        qkv_kernel,
        grid_spec=pltpu.PrefetchScalarGridSpec(
            num_scalar_prefetch=1,
            grid=(rows // step,),
            in_specs=[block(256)] * 3
            + [
                pl.BlockSpec((step, 256), lambda i, s: (jnp.minimum(i, last), 0)),
                pl.BlockSpec((step, 256), lambda i, s: (jnp.maximum(i - last - 1, 0), 0)),
            ]
            + [
                whole(gains.shape),
                whole(w_own.shape),
                pl.BlockSpec((step, 128), lambda i, s: (s[1] * (rows // step) + i, 0)),
            ],
            out_specs=[block(384), block(1024), block(128), whole((step, 1024))],
            scratch_shapes=[pltpu.VMEM((step, 256), BF16)],
        ),
        out_shape=[
            shape(384), shape(1024), shape(128, F32), jax.ShapeDtypeStruct((step, 1024), BF16),
        ],
        compiler_params=room(20),
        cost_estimate=COST,
    )(index, *xs, gains, w_own, table)


def run_away(index, h, w_own, table):
    rows = h.shape[0]
    block = lambda n: pl.BlockSpec((256, n), lambda i, s: (i, 0))
    return pl.pallas_call(
        away_kernel,
        grid_spec=pltpu.PrefetchScalarGridSpec(
            num_scalar_prefetch=1,
            grid=(rows // 256,),
            in_specs=[
                block(1024),
                pl.BlockSpec(w_own.shape, lambda i, s: (0, 0, 0)),
                pl.BlockSpec((256, 128), lambda i, s: ((1 - s[1]) * (rows // 256) + i, 0)),
            ],
            out_specs=block(384),
        ),
        out_shape=jax.ShapeDtypeStruct((rows, 384), BF16),
        compiler_params=room(16),
        cost_estimate=COST,
    )(index, h, w_own, table)


def to_columns(row):
    return jnp.transpose(jnp.broadcast_to(row, (LANES, row.shape[1])))


def attend_kernel(info, seg, own, recv, own_out, oth_out, lse_out, qkv, mixed, seg_col, sems):
    length = qkv.shape[0]
    rows = length // 2
    blocks = length // BLOCK
    here = info[4, 0]
    mine = pl.ds(pl.multiple_of(here * rows, rows), rows)
    other = pl.ds(pl.multiple_of((1 - here) * rows, rows), rows)
    copies = [
        pltpu.make_async_copy(own, qkv.at[mine, :], sems.at[0]),
        pltpu.make_async_copy(recv, qkv.at[other, :], sems.at[1]),
    ]
    for copy in copies:
        copy.start()
    for i in range(blocks):
        seg_col[i * BLOCK : (i + 1) * BLOCK, :] = to_columns(seg[:, i * BLOCK : (i + 1) * BLOCK])
    for copy in copies:
        copy.wait()
    low_half = half_mask((BLOCK, LANES))
    zero = jnp.zeros((BLOCK, LANES), BF16)

    def wide_block(at, first, count):
        query = qkv[pl.ds(at, BLOCK), :128]
        pair = jnp.concatenate(
            [jnp.where(low_half, query, zero), jnp.where(low_half, zero, query)], axis=0
        )
        k_at = pl.multiple_of(jnp.minimum(first, blocks - count) * BLOCK, BLOCK)
        span = pl.ds(k_at, count * BLOCK)
        got = mm(pair, qkv[span, 128:256], NT)
        seg_q = seg_col[pl.ds(at, BLOCK), :]
        seg_k = seg[:, span]
        chunks = []
        for j in range(count * 2):
            lanes = slice(j * LANES, (j + 1) * LANES)
            same = seg_q == seg_k[:, lanes]
            chunks.append(
                [
                    jnp.where(same, got[:BLOCK, lanes], MASKED),
                    jnp.where(same, got[BLOCK:, lanes], MASKED),
                ]
            )
        mixing, lse = [], []
        weights = []
        for head in range(2):
            highest = chunks[0][head]
            for j in range(1, count * 2):
                highest = jnp.maximum(highest, chunks[j][head])
            highest = jnp.max(highest, axis=1, keepdims=True)
            weight = [jnp.exp(chunks[j][head] - highest) for j in range(count * 2)]
            total = weight[0]
            for j in range(1, count * 2):
                total = total + weight[j]
            total = jnp.sum(total, axis=1, keepdims=True)
            weights.append(jnp.concatenate([w.astype(BF16) for w in weight], axis=1))
            mixing.append(total)
            lse.append(highest + jnp.log(total))
        both = mm(jnp.concatenate(weights, axis=0), qkv[span, 256:], NN)
        mixed[pl.ds(at, BLOCK), :] = jnp.where(
            low_half, both[:BLOCK] / mixing[0], both[BLOCK:] / mixing[1]
        ).astype(BF16)
        for head in range(2):
            lse_out[head : head + 1, pl.ds(at, BLOCK)] = to_row_form(lse[head])

    def one_block(qb, _):
        at = pl.multiple_of(qb * BLOCK, BLOCK)
        first = info[0, qb]
        need = info[1, qb] - first
        sizes = SIZES
        for i, count in enumerate(sizes):
            least = sizes[i - 1] if i else 0

            @pl.when((need > least) & (need <= count))
            def _(count=count):
                wide_block(at, first, count)

        return 0

    lax.fori_loop(0, blocks, one_block, 0)
    own_out[...] = mixed[pl.ds(pl.multiple_of(here * rows, rows), rows), :]
    oth_out[...] = mixed[pl.ds(pl.multiple_of((1 - here) * rows, rows), rows), :]


def attend_back_kernel(
    info, seg, lse, dm_own, dm_recv, mix_own, mix_oth, own, recv, table_from,
    own_out, oth_out, qkv, dmix, dsum, dquery, dout, seg_col, table, mixed, sems,
):
    length = qkv.shape[0]
    rows = length // 2
    here = info[4, 0]
    mine = pl.ds(pl.multiple_of(here * rows, rows), rows)
    other = pl.ds(pl.multiple_of((1 - here) * rows, rows), rows)
    early = [
        pltpu.make_async_copy(mix_own, mixed.at[mine, :], sems.at[3]),
        pltpu.make_async_copy(mix_oth, mixed.at[other, :], sems.at[4]),
    ]
    copies = [
        pltpu.make_async_copy(own, qkv.at[mine, :], sems.at[0]),
        pltpu.make_async_copy(recv, qkv.at[other, :], sems.at[1]),
        pltpu.make_async_copy(table_from, table, sems.at[2]),
    ]
    for copy in early + copies:
        copy.start()
    dmix[mine, :] = dm_own[...]
    dmix[other, :] = dm_recv[...]
    blocks = length // BLOCK
    for i in range(blocks):
        seg_col[i * BLOCK : (i + 1) * BLOCK, :] = to_columns(seg[:, i * BLOCK : (i + 1) * BLOCK])

    for copy in early:
        copy.wait()

    def inner(qb, _):
        at = pl.multiple_of(qb * BLOCK, BLOCK)
        block = pl.ds(at, BLOCK)
        product = jnp.transpose(dmix[block, :].astype(F32) * mixed[block, :].astype(F32))
        dsum[0:1, pl.ds(at, BLOCK)] = jnp.sum(product[:64], axis=0, keepdims=True)
        dsum[1:2, pl.ds(at, BLOCK)] = jnp.sum(product[64:], axis=0, keepdims=True)
        dquery[pl.ds(at, BLOCK), :] = jnp.zeros((BLOCK, LANES), F32)
        return 0

    lax.fori_loop(0, blocks, inner, 0)
    for copy in copies:
        copy.wait()
    low_half = half_mask((BLOCK, LANES))
    zero = jnp.zeros((BLOCK, LANES), BF16)

    def both(v):
        return jnp.concatenate([jnp.where(low_half, v, zero), jnp.where(low_half, zero, v)], axis=0)

    def wide_block(k_at, first, count):
        key_pair = both(qkv[pl.ds(k_at, BLOCK), 128:256])
        value_pair = both(qkv[pl.ds(k_at, BLOCK), 256:])
        seg_k = seg_col[pl.ds(k_at, BLOCK), :]
        at = pl.multiple_of(jnp.minimum(first, blocks - count) * BLOCK, BLOCK)
        span = pl.ds(at, count * BLOCK)
        query, grad = qkv[span, :128], dmix[span, :]
        got = mm(key_pair, query, NT)
        dgot = mm(value_pair, grad, NT)
        lse_q, dsum_q, seg_q = lse[:, span], dsum[:, span], seg[:, span]
        weights, dscores = [], []
        for head in range(2):
            rows_h = slice(head * BLOCK, (head + 1) * BLOCK)
            weight_h, dscore_h = [], []
            for j in range(count * 2):
                lanes = slice(j * LANES, (j + 1) * LANES)
                same = seg_k == seg_q[:, lanes]
                weight = jnp.exp(
                    jnp.where(same, got[rows_h, lanes] - lse_q[head : head + 1, lanes], MASKED)
                )
                weight_h.append(weight.astype(BF16))
                dscore_h.append(
                    (weight * (dgot[rows_h, lanes] - dsum_q[head : head + 1, lanes])).astype(BF16)
                )
            weights.append(jnp.concatenate(weight_h, axis=1))
            dscores.append(jnp.concatenate(dscore_h, axis=1))
        weights = jnp.concatenate(weights, axis=0)
        dscores = jnp.concatenate(dscores, axis=0)
        dvalue = mm(weights, grad, NN)
        dkey = mm(dscores, query, NN)
        dquery[span, :] += jnp.transpose(mm(key_pair, dscores, TN))
        dkey = jnp.where(low_half, dkey[:BLOCK], dkey[BLOCK:])
        dvalue = jnp.where(low_half, dvalue[:BLOCK], dvalue[BLOCK:])
        cos_part, sin_part = rope_of(table[pl.ds(k_at, BLOCK), :])
        dkey = dkey * cos_part - swap_halves(dkey) * sin_part
        dout[pl.ds(k_at, BLOCK), 128:256] = dkey.astype(BF16)
        dout[pl.ds(k_at, BLOCK), 256:] = dvalue.astype(BF16)

    def one_block(kb, _):
        k_at = pl.multiple_of(kb * BLOCK, BLOCK)
        first = info[0, kb]
        need = info[1, kb] - first
        for i, count in enumerate(SIZES):
            least = SIZES[i - 1] if i else 0

            @pl.when((need > least) & (need <= count))
            def _(count=count):
                wide_block(k_at, first, count)

        return 0

    lax.fori_loop(0, blocks, one_block, 0)

    def finish(qb, _):
        at = pl.multiple_of(qb * BLOCK, BLOCK)
        cos_part, sin_part = rope_of(table[pl.ds(at, BLOCK), :])
        grad = dquery[pl.ds(at, BLOCK), :] * 0.125
        grad = grad * cos_part - swap_halves(grad) * sin_part
        dout[pl.ds(at, BLOCK), :128] = grad.astype(BF16)
        return 0

    lax.fori_loop(0, blocks, finish, 0)
    own_out[...] = dout[mine, :]
    oth_out[...] = dout[other, :]


def run_attend(info, own, recv, seg_row):
    rows, length = own.shape[0], seg_row.shape[1]
    return whole_call(
        attend_kernel,
        [((rows, LANES), BF16), ((rows, LANES), BF16), ((2, length), F32)],
        (info, seg_row, own, recv),
        [
            pltpu.VMEM((length, 384), BF16),
            pltpu.VMEM((length, LANES), BF16),
            pltpu.VMEM((length, LANES), F32),
            pltpu.SemaphoreType.DMA((2,)),
        ],
        away=2,
        extra=46,
    )


def run_attend_back(
    info, own, recv, seg_row, lse, mix_own, mix_away, dm_own, dm_recv, table
):
    rows, length = own.shape[0], seg_row.shape[1]
    return whole_call(
        attend_back_kernel,
        [((rows, 384), BF16), ((rows, 384), BF16)],
        (info, seg_row, lse, dm_own, dm_recv, mix_own, mix_away, own, recv, table),
        [
            pltpu.VMEM((length, 384), BF16),
            pltpu.VMEM((length, LANES), BF16),
            pltpu.VMEM((2, length), F32),
            pltpu.VMEM((length, LANES), F32),
            pltpu.VMEM((length, 384), BF16),
            pltpu.VMEM((length, LANES), F32),
            pltpu.VMEM((length, LANES), F32),
            pltpu.VMEM((length, LANES), BF16),
            pltpu.SemaphoreType.DMA((5,)),
        ],
        extra=36,
        away=5,
    )


def slot_rows(info, k):
    return pl.ds(pl.multiple_of((info[4, 1] ^ k) * 256, 256), 256)


def attn_out_kernel(plan, info, mix_own, mix_oth, w_own, w_oth, *outs):
    for out, pieces in zip(outs, plan):
        at = 0
        for k, first, count in pieces:
            start = pl.multiple_of((info[4, 1] ^ k) * 256 + first, 128)
            rows = pl.ds(start, count)
            mix = jnp.concatenate([mix_own[rows, :], mix_oth[rows, :]], axis=1)
            for p in range(4):
                weight = jnp.concatenate([w_own[k ^ p, 384:512], w_oth[k ^ p, 384:512]], axis=0)
                out[at : at + count, p * 256 : (p + 1) * 256] = mm(mix, weight, NN).astype(BF16)
            at += count


def relay_kernel(first, x, p0, got, part, sent_out, kept_out):
    half = got.shape[0] // 2
    sent_out[...] = (part[...].astype(F32) + got[half:, :].astype(F32)).astype(BF16)
    rows = slice(first, first + half)
    kept_out[...] = x[rows, :].astype(F32) + p0[rows, :].astype(F32) + got[:half, :].astype(F32)


def middle_kernel(kept_a, got_a, kept_b, got_b, out):
    half = kept_a.shape[0]
    out[:half, :] = (kept_a[...] + got_a[...].astype(F32)).astype(BF16)
    out[half:, :] = (kept_b[...] + got_b[...].astype(F32)).astype(BF16)


def ffn_kernel(k, index, *refs):
    pieces = 2 if k == 3 else 1
    part = jnp.concatenate([ref[...] for ref in refs[:pieces]], axis=0)
    d0, d1, d2, d3, gains, w_own, w_oth, *refs = refs[pieces:]
    backs = refs[-pieces:]
    f0, f1, f2, f3, h_out, hid_out, dug_out, mid_out = refs[-8 - pieces : -pieces]
    parts = [part[:, (k ^ p) * 256 : ((k ^ p) + 1) * 256] for p in range(4)]
    mid_out[...] = parts[0]
    units, _ = moments([v.astype(F32) for v in parts], 4 * 256)
    low = [(units[p] * gains[p, 1:2, :]).astype(BF16) for p in range(4)]
    for p in range(4):
        h_out[:, p * 256 : (p + 1) * 256] = low[p]
    grads = [ref[...] for ref in (d0, d1, d2, d3)]

    def weight(p, i):
        rows = slice(i * 384, (i + 1) * 384)
        return jnp.concatenate([w_own[p, rows], w_oth[p, rows]], axis=0)

    gate = sum(mm(low[p], weight(p, 0), NT) for p in range(4))
    up = sum(mm(low[p], weight(p, 1), NT) for p in range(4))
    dhidden = sum(mm(grads[p], weight(p, 2), NT) for p in range(4))
    phi = 0.5 * (1.0 + lax.erf(gate * (2.0**-0.5)))
    density = jnp.exp(-0.5 * gate * gate) * ((2.0 * math.pi) ** -0.5)
    act = gate * phi
    hidden = (act * up).astype(BF16)
    dgate = (dhidden * up * (phi + gate * density)).astype(BF16)
    dup = (dhidden * act).astype(BF16)
    hid_out[...] = hidden
    dug_out[:, :384] = dgate[:, :384]
    dug_out[:, 384:768] = dup[:, :384]
    dug_out[:, 768:1152] = dgate[:, 384:]
    dug_out[:, 1152:] = dup[:, 384:]
    for p in range(4):
        got = mm(dgate, weight(p, 0), NN) + mm(dup, weight(p, 1), NN)
        got = got.astype(BF16)
        for i, out in enumerate(backs):
            out[:, (k ^ p) * 256 : ((k ^ p) + 1) * 256] = got[i * (256 // pieces) : (i + 1) * (256 // pieces)]
    for p, out in enumerate((f0, f1, f2, f3)):
        out[...] = mm(hidden, weight(p, 2), NN).astype(BF16)


def run_ffn(k, index, mids, grads, gains, w_own, w_oth, held):
    rows = grads[0].shape[0]
    whole = lambda shape: pl.BlockSpec(shape, lambda i, s: (0,) * len(shape))
    block = lambda n: pl.BlockSpec((256, n), lambda i, s: (s[0] ^ k, 0))
    widths = [256] * 4 + [1024, 768, 1536, 256]
    outs = pl.pallas_call(
        functools.partial(ffn_kernel, k),
        grid_spec=pltpu.PrefetchScalarGridSpec(
            num_scalar_prefetch=1,
            grid=(1,),
            in_specs=[whole(v.shape) for v in mids]
            + [block(256)] * 4
            + [whole(gains.shape), whole(w_own.shape), whole(w_oth.shape)]
            + [pl.BlockSpec(memory_space=pl.ANY)] * len(held),
            out_specs=[block(n) for n in widths] + [whole(v.shape) for v in mids],
        ),
        out_shape=[jax.ShapeDtypeStruct((rows, n), BF16) for n in widths]
        + [jax.ShapeDtypeStruct(v.shape, BF16) for v in mids],
        input_output_aliases={8 + len(mids) + i: i for i in range(len(held))},
        compiler_params=room(26),
        cost_estimate=COST,
    )(index, *mids, *grads, gains, w_own, w_oth, *held)
    return outs[:8], list(outs[8:])


def pack_kernel(*refs):
    out = refs[-1]
    planes, _, rows, _ = out.shape
    for p in range(4):
        block = slice(p * 256, (p + 1) * 256)
        total = sum(ref[block, :].astype(F32) for ref in refs[:-1]).astype(BF16)
        for d in range(planes):
            out[d, p] = total[d * rows : (d + 1) * rows]


def pack_dp(*terms):
    planes, width = lax.axis_size("dp"), terms[0].shape[1]
    if planes > 16:
        total = sum(v.astype(F32) for v in terms).astype(BF16)
        return jnp.swapaxes(total.reshape(4, planes, 256 // planes, width), 0, 1)
    return whole_call(
        pack_kernel, [((planes, 4, 256 // planes, width), BF16)], terms, scalars=0
    )[0]


def norm_back(grads, units, inverse, gains):
    scaled = [g * w for g, w in zip(grads, gains)]
    first = sum(jnp.sum(v, axis=1, keepdims=True) for v in scaled) / 1024
    second = sum(jnp.sum(v * u, axis=1, keepdims=True) for v, u in zip(scaled, units)) / 1024
    return [inverse * (v - first - u * second) for v, u in zip(scaled, units)]


def middle_back_kernel(info, mid, p0, p1, p2, p3a, p3b, d0, d1, d2, d3, gains, dx_out, dz_out, gain_out):
    rows = slot_rows(info, 0)
    at = [slice(p * 256, (p + 1) * 256) for p in range(4)]
    units, inverse = moments([mid[:, a].astype(F32) for a in at], 1024)
    last = jnp.concatenate([p3a[...], p3b[...]], axis=0)
    grads = [sum(part[:, a].astype(F32) for part in (p0, p1, p2, last)) for a in at]
    back = norm_back(grads, units, inverse, [gains[p, 1:2, :] for p in range(4)])
    for p, dy in enumerate((d0, d1, d2, d3)):
        total = back[p] + dy[rows, :].astype(F32)
        dx_out[:, at[p]] = total
        dz_out[:, at[p]] = total.astype(BF16)
        gain_out[p : p + 1, :] = jnp.sum(grads[p] * units[p], axis=0, keepdims=True)


def mixed_back_kernel(k, index, *refs):
    pieces = 2 if k == 3 else 1
    part = jnp.concatenate([ref[...] for ref in refs[:pieces]], axis=0)
    w_own, w_oth = refs[pieces : pieces + 2]
    own_out, oth_out, dz_out = refs[-3:]
    total = None
    for p in range(4):
        piece = part[:, (k ^ p) * 256 : ((k ^ p) + 1) * 256]
        dz_out[:, p * 256 : (p + 1) * 256] = piece
        term = mm(piece, jnp.concatenate([w_own[p], w_oth[p]], axis=0), NT)
        total = term if total is None else total + term
    own_out[...] = total[:, :128].astype(BF16)
    oth_out[...] = total[:, 128:].astype(BF16)


def run_mixed_back(k, index, parts, w_own, w_oth, held):
    rows = 4 * 256
    whole = lambda shape: pl.BlockSpec(shape, lambda i, s: (0,) * len(shape))
    block = lambda n: pl.BlockSpec((256, n), lambda i, s: (s[0] ^ k, 0))
    weight = pl.BlockSpec((4, 128, 256), lambda i, s: (0, 3, 0))
    return pl.pallas_call(
        functools.partial(mixed_back_kernel, k),
        grid_spec=pltpu.PrefetchScalarGridSpec(
            num_scalar_prefetch=1,
            grid=(1,),
            in_specs=[whole(v.shape) for v in parts]
            + [weight, weight]
            + [pl.BlockSpec(memory_space=pl.ANY)] * len(held),
            out_specs=[block(128), block(128), block(1024)],
        ),
        out_shape=[jax.ShapeDtypeStruct((rows, n), BF16) for n in (128, 128, 1024)],
        input_output_aliases={3 + len(parts) + i: i for i in range(len(held))},
        compiler_params=room(12),
        cost_estimate=COST,
    )(index, *parts, w_own, w_oth, *held)


def to_row_form(column):
    return jnp.transpose(jnp.broadcast_to(column, (column.shape[0], LANES)))[0:1, :]


def input_back_kernel(d_own, d_oth, w_own, w_oth, h, gains, o0, o1, o2, o3, sums_out, gain_out):
    step = pl.program_id(0)
    grad = jnp.concatenate([d_own[...], d_oth[...]], axis=1)
    first = second = None
    for p, out in enumerate((o0, o1, o2, o3)):
        weight = jnp.concatenate([w_own[p, :384], w_oth[p, :384]], axis=0)
        got = mm(grad, weight, NN)
        out[...] = got.astype(BF16)
        crossed = got * h[:, p * 256 : (p + 1) * 256].astype(F32)
        scaled = got * gains[p, 0:1, :]
        scaled = scaled[:, :128] + scaled[:, 128:]
        across = crossed[:, :128] + crossed[:, 128:]
        first = scaled if first is None else first + scaled
        second = across if second is None else second + across
        part = jnp.sum(crossed, axis=0, keepdims=True) / gains[p, 0:1, :]

        @pl.when(step == 0)
        def _():
            gain_out[p : p + 1, :] = part

        @pl.when(step > 0)
        def _():
            gain_out[p : p + 1, :] += part

    sums_out[0:1, :] = jnp.sum(jnp.transpose(first), axis=0, keepdims=True)
    sums_out[1:2, :] = jnp.sum(jnp.transpose(second), axis=0, keepdims=True)


def run_input_back(d_own, d_oth, w_own, w_oth, h, gains):
    rows = h.shape[0]
    whole = lambda shape: pl.BlockSpec(shape, lambda i: (0,) * len(shape))
    block = lambda n: pl.BlockSpec((256, n), lambda i: (i, 0))
    return pl.pallas_call(
        input_back_kernel,
        grid=(rows // 256,),
        in_specs=[block(384), block(384), whole(w_own.shape), whole(w_oth.shape), block(1024), whole(gains.shape)],
        out_specs=[block(256)] * 4 + [pl.BlockSpec((2, 256), lambda i: (0, i)), whole((4, 256))],
        out_shape=[jax.ShapeDtypeStruct((rows, 256), BF16)] * 4
        + [jax.ShapeDtypeStruct((2, rows), F32), jax.ShapeDtypeStruct((4, 256), F32)],
        compiler_params=room(24),
        cost_estimate=COST,
    )(d_own, d_oth, w_own, w_oth, h, gains)


def input_grad_kernel(p0, p1, p2, p3, sums, h, dz, inv, gains, out):
    first = to_columns(sums[0:1, :]) / 1024
    second = to_columns(sums[1:2, :]) / 1024
    both = lambda v: jnp.concatenate([v, v], axis=1)
    gain = gains[0, 0:1, :]
    total = sum(ref[...].astype(F32) for ref in (p0, p1, p2, p3)) * gain
    unit = h[...].astype(F32) / gain
    out[...] = dz[...].astype(F32) + both(inv[...]) * (total - both(first) - unit * both(second))


def run_input_grad(parts, sums, h, dz, inv, gains):
    rows = h.shape[0]
    block = lambda n: pl.BlockSpec((256, n), lambda i: (i, 0))
    return pl.pallas_call(
        input_grad_kernel,
        grid=(rows // 256,),
        in_specs=[block(256)] * 4
        + [pl.BlockSpec((2, 256), lambda i: (0, i)), block(256), block(256), block(128)]
        + [pl.BlockSpec(gains.shape, lambda i: (0, 0, 0))],
        out_specs=block(256),
        out_shape=jax.ShapeDtypeStruct((rows, 256), F32),
        compiler_params=room(12),
        cost_estimate=COST,
    )(*parts, sums, h, dz, inv, gains)


def adam_update(master, first_moment, second, gradient, factor, decay_rate, step_rate):
    scaled = gradient * factor
    first_new = BETA_ONE * first_moment + (1.0 - BETA_ONE) * scaled
    second_new = BETA_TWO * second + (1.0 - BETA_TWO) * scaled * scaled
    first_hat = first_new / (1.0 - BETA_ONE**STEP)
    second_hat = second_new / (1.0 - BETA_TWO**STEP)
    master_new = master - step_rate * (
        first_hat / (jnp.sqrt(second_hat) + ADAM_EPSILON) + decay_rate * master
    )
    return (first_new, second_new, master_new)


def positions(segment):
    length = segment.shape[0]
    number = jnp.arange(length, dtype=jnp.int32)
    before = jnp.concatenate([segment[:1] - 1, segment[:-1]])
    change_marks = jnp.where(segment != before, number, jnp.zeros_like(number))
    return number - lax.cummax(change_marks, axis=0)


def rope_table(place):
    lane = jnp.arange(LANES) % 64
    frequency = ROPE_BASE ** (-(2.0 * (lane % 32).astype(F32)) / 64)
    turned = place.astype(F32)[:, None] * frequency[None, :]
    return jnp.where(lane[None, :] < 32, jnp.cos(turned), jnp.sin(turned))


def on_device(
    tokens, segment_ids, cotangent, qkv_weight, attn_weight, in_weight, out_weight, norm_gains,
    qkv_master, attn_master, in_master, out_master,
    qkv_first, attn_first, in_first, out_first,
    qkv_second, attn_second, in_second, out_second,
    gains_first, gains_second,
):
    col, row = lax.axis_index("col"), lax.axis_index("row")
    segment = segment_ids[0]
    length = segment.shape[0]
    rows = length // 2
    blocks = length // BLOCK
    ff_here = in_weight.shape[2] // 4
    ff_pad = -ff_here % FF_PAD
    ff_wide = ff_here + ff_pad

    qkv_t = jnp.transpose(qkv_weight, (1, 2, 3, 0))
    attn_t = attn_weight.reshape(4, LANES, 256)
    in_t = jnp.transpose(in_weight, (1, 2, 0)).reshape(2, 4, ff_here, 256)
    out_t = out_weight.reshape(4, ff_here, 256)

    index = jnp.stack([col, row])
    a = to_col(tokens, 1)
    b = to_col(tokens, 2)
    high = norm_gains.astype(BF16)
    rest = norm_gains - high.astype(F32)
    middle = rest.astype(BF16)
    lowest = (rest - middle.astype(F32)).astype(BF16)
    gain_rows = jnp.concatenate([high, middle, lowest, jnp.zeros((10, 256), BF16)], axis=0)
    gain_rows = lax.optimization_barrier(gain_rows)

    def wide_piece(k):
        qkv = lax.dynamic_slice_in_dim(qkv_t, 2 * (col ^ k), 2, 1).reshape(3 * LANES, 256)
        return jnp.concatenate(
            [qkv, lax.dynamic_index_in_dim(attn_t, col ^ k, 0, keepdims=False), gain_rows], axis=0
        )

    half = tokens.shape[0] // 2
    x3a, x3b = to_col(a[:half], 2), to_col(b[half:], 1)
    xs = [tokens, a, b, x3a, x3b]
    wa_parts = exchange_col([wide_piece(k) for k in range(4)])
    wa_own = jnp.stack(after(wa_parts, x3a, x3b))
    ff_gate = (x3a, x3b)
    gains = wa_own[:, 512:518].astype(F32).reshape(4, 3, 2, 256)
    gains = gains[:, 0] + gains[:, 1] + gains[:, 2]

    planes = lax.axis_size("dp")
    fill = [(0, 0), (0, 0), (0, ff_pad), (0, 0)]
    ff_t = jnp.pad(jnp.concatenate([in_t, out_t[None]], axis=0), fill)
    ff_t = ff_t.reshape(3, 4, planes, ff_wide // planes, 256)
    ff_t = lax.dynamic_index_in_dim(ff_t, lax.axis_index("dp"), 2, keepdims=False)
    ff_parts = [lax.dynamic_index_in_dim(ff_t, col ^ k, 1, keepdims=False) for k in range(4)]
    ff_parts = exchange_col(after(ff_parts, *ff_gate))
    first = segment[::BLOCK]
    last = segment[BLOCK - 1 :: BLOCK]
    low = jnp.sum((segment[None, :] < first[:, None]).astype(jnp.int32), axis=1) // BLOCK
    high = (
        jnp.sum((segment[None, :] <= last[:, None]).astype(jnp.int32), axis=1) + BLOCK - 1
    ) // BLOCK
    place_here = jnp.zeros((blocks,), jnp.int32).at[0].set(row).at[1].set(col)
    info = jnp.stack([low, high, first, last, place_here])
    seg_row = segment_ids.astype(F32)
    table = rope_table(positions(segment))
    own, h1, inv, x_slot = run_qkv(index, xs, gains, wa_own, table)
    h1_recv = to_row(h1)
    dys = exchange_col([after(cotangent, own)] * 4)
    wa_oth = to_row(after(wa_own, own))
    ff_own = lax.all_gather(jnp.stack(after(ff_parts, own)), "dp", axis=2)
    recv = run_away(index, h1_recv, wa_own, table)
    mix_own, mix_away, lse = run_attend(info, own, recv, seg_row)
    mix_own, mix_away, lse, dys, wa_oth = after((mix_own, mix_away, lse, dys, wa_oth), wa_oth)
    mix_oth = to_row(mix_away)
    def attn_out(*plan):
        return whole_call(
            functools.partial(attn_out_kernel, plan),
            [((sum(count for _, _, count in pieces), 1024), BF16) for pieces in plan],
            (info, mix_own, mix_oth, wa_own, wa_oth),
        )

    x_first, y_first = attn_out(((1, 0, 128), (3, 0, 128)), ((2, 128, 128), (3, 128, 128)))
    x_first, y_first = to_col(x_first, 1), to_col(y_first, 2)
    x_part, y_part, part = attn_out(((1, 128, 128),), ((2, 0, 128),), ((0, 0, 256),))
    relay = lambda first, got, mine: whole_call(
        functools.partial(relay_kernel, first),
        [((128, 1024), BF16), ((128, 1024), F32)],
        (x_slot, part, got, mine),
        scalars=0,
    )
    y_second, kept_a = relay(0, x_first, y_part)
    x_second, kept_b = relay(128, y_first, x_part)
    y_second, x_second = to_col(y_second, 2), to_col(x_second, 1)
    (middle,) = whole_call(
        middle_kernel, [((256, 1024), BF16)], (kept_a, y_second, kept_b, x_second), scalars=0
    )
    ff_own = after(ff_own, x_second, y_second).reshape(4, 3 * ff_wide, 256)
    ff_oth = to_row(ff_own)
    m1, m2 = to_col(middle, 1), to_col(middle, 2)
    m3a, m3b = to_col(m1[:128], 2), to_col(m2[128:], 1)
    held, backward = (), [None] * 4
    for k, mids in enumerate(((middle,), (m1,), (m2,), (m3a, m3b))):
        held, part = run_ffn(k, index, mids, dys, gains, ff_own, ff_oth, held)
        backward[k] = [to_col(v, k) for v in part] if k else part
    forward = held[:4]
    h2, hidden, dug, mid_here = held[4:]
    dx_mid, dz, gain_two = whole_call(
        middle_back_kernel,
        [((256, 1024), F32), ((256, 1024), BF16), ((4, 256), F32)],
        (info, middle, *sum(backward, []), *dys, gains),
    )
    z1, z2 = to_col(dz, 1), to_col(dz, 2)
    z3a, z3b = to_col(z1[:128], 2), to_col(z2[128:], 1)

    h2, hidden, dug = after((h2, hidden, dug), z1, z2)
    dy_all = jnp.concatenate(dys, axis=1)
    ffn_own, ffn_oth = (
        jnp.concatenate(
            [
                mm(h2, dug[:, i * 2 * ff_wide : (i + 1) * 2 * ff_wide], TN).astype(BF16),
                mm(dy_all, hidden[:, i * ff_wide : (i + 1) * ff_wide], TN).astype(BF16),
            ],
            axis=1,
        )
        for i in range(2)
    )
    ffn_oth = to_row(ffn_oth)
    ffn_oth, z3a, z3b = after((ffn_oth, z3a, z3b), z3a, z3b)
    ffn_grad = lax.psum_scatter(pack_dp(ffn_own, ffn_oth), "dp", scatter_dimension=0).astype(F32)

    held = ()
    for k, parts in enumerate(((dz,), (z1,), (z2,), (z3a, z3b))):
        held = run_mixed_back(k, index, parts, wa_own, wa_oth, held)
    dm_own, dm_away, dz_here = held
    dm_recv = to_row(dm_away)
    forward = exchange_col(after(forward, dm_own))
    dq_own, dq_away = run_attend_back(
        info, own, recv, seg_row, lse, mix_own, mix_away, dm_own, dm_recv, table
    )
    dq_own, dq_away, forward, dz_here = after((dq_own, dq_away, forward, dz_here), forward[1:])
    layer_out = (mid_here.astype(F32) + sum(v.astype(F32) for v in forward)).astype(BF16)
    dq_oth = to_row(dq_away)

    attn_both = mm(dz_here, jnp.concatenate([mix_own, mix_oth], axis=1), TN)
    attn_sent = to_row(attn_both[:, LANES:].astype(BF16))
    attn_sum = (attn_both[:, :LANES] + attn_sent.astype(F32)).astype(BF16)
    qkv_sum = (mm(h1, dq_own, TN) + mm(h1_recv, dq_away, TN)).astype(BF16)

    *partial_first, sums, gain_one = run_input_back(dq_own, dq_oth, wa_own, wa_oth, h1, gains)
    notes = [
        jnp.concatenate([sums, jnp.pad(jnp.stack([gain_one[k], gain_two[k]]), [(0, 0), (0, rows - 256)])])
        for k in range(4)
    ]
    late = after(pack_dp(jnp.concatenate([qkv_sum, attn_sum], axis=1)), gain_one)
    late = scatter_dp(late)
    notes = exchange_col(notes)
    partial_first = exchange_col(after(partial_first, notes[1]))
    note = sum(notes)
    input_grad = run_input_grad(partial_first, note[:2], h1, dz_here, inv, gains)

    early = ffn_grad.astype(BF16)
    early = natural(exchange_col([early[k] for k in range(4)]), col)
    late = after(late, early, *partial_first[1:])
    squares = jnp.sum(ffn_grad * ffn_grad) + jnp.sum(late * late)
    message = jnp.concatenate([note[2:, :256], jnp.full((6, 256), squares)], axis=0)
    message = sum_dp(message)
    message = message + to_row(message)
    gain_grad = message[:2]
    total = message[2:3, :LANES] + jnp.sum(gain_grad * gain_grad)
    total = jnp.broadcast_to(total, (8, LANES))
    total = sum(exchange_col([total] * 4))
    grad_norm = jnp.sqrt(total[0, 0])
    factor = CLIP_NORM / (grad_norm + 1e-06)

    shard = late.shape[1]
    late = late.astype(BF16)
    late = natural(exchange_col([late[k] for k in range(4)]), col)
    grad_qkv = jnp.stack([v[:, : 3 * LANES].reshape(shard, 3, 2, 64) for v in late], axis=2).reshape(
        qkv_master.shape
    )
    grad_attn = jnp.concatenate([v[:, 3 * LANES :] for v in late], axis=1).T.reshape(
        attn_master.shape
    )
    grad_in = jnp.stack(
        [
            jnp.concatenate([v[:, i * ff_wide : i * ff_wide + ff_here] for v in early], axis=1)
            for i in range(2)
        ],
        axis=1,
    )
    grad_out = jnp.concatenate([v[:, 2 * ff_wide : 2 * ff_wide + ff_here] for v in early], axis=1).T

    grad_qkv, grad_attn, grad_in, grad_out = (
        v.astype(F32) for v in (grad_qkv, grad_attn, grad_in, grad_out)
    )
    qkv_new = adam_update(
        qkv_master, qkv_first, qkv_second, grad_qkv, factor, WEIGHT_DECAY, LEARN_RATE
    )
    attn_new = adam_update(
        attn_master, attn_first, attn_second, grad_attn, factor, WEIGHT_DECAY, LEARN_RATE
    )
    in_new = adam_update(in_master, in_first, in_second, grad_in, factor, WEIGHT_DECAY, LEARN_RATE)
    out_new = adam_update(
        out_master, out_first, out_second, grad_out, factor, WEIGHT_DECAY, LEARN_RATE
    )
    gains_new = adam_update(
        norm_gains, gains_first, gains_second, gain_grad, factor, 0.0, GAIN_RATE
    )
    return (
        layer_out, input_grad, grad_norm,
        qkv_new[0], attn_new[0], in_new[0], out_new[0],
        qkv_new[1], attn_new[1], in_new[1], out_new[1],
        qkv_new[2], attn_new[2], in_new[2], out_new[2],
        qkv_new[2].astype(BF16), attn_new[2].astype(BF16),
        in_new[2].astype(BF16), out_new[2].astype(BF16),
        gains_new[0], gains_new[1], gains_new[2],
    )


def solution(mesh):
    activations = P(("dp", "row"), "col")
    gains = P(None, "col")
    weights = (
        P("col", None, "row", None), P("row", None, "col"), P("col", None, "row"), P("row", "col"),
    )
    states = (
        P(("col", "dp"), None, "row", None), P("row", None, ("col", "dp")),
        P(("col", "dp"), None, "row"), P("row", ("col", "dp")),
    )
    return jax.shard_map(
        on_device,
        mesh=mesh,
        in_specs=(activations, P("dp", None), activations, *weights, gains)
        + states * 3
        + (gains, gains),
        out_specs=(activations, activations, P()) + states * 4 + (gains, gains, gains),
        check_vma=False,
    )
```

```python
import functools
import math

import jax
import jax.numpy as jnp
from jax import lax
from jax.experimental import pallas as pl
from jax.experimental.pallas import tpu as pltpu
from jax.sharding import PartitionSpec as P

STEP = 10


NORM_EPSILON = 1e-05
ROPE_BASE = 160000.0
CLIP_NORM = 1.0
LEARN_RATE = 0.02
GAIN_RATE = 0.5
BETA_ONE = 0.9
BETA_TWO = 0.98
ADAM_EPSILON = 1e-08
WEIGHT_DECAY = 0.01
MASKED = -1e30
SIZES = (1, 2, 3, 4, 5, 6, 7, 8)

BLOCK = 256
LANES = 128
FF_PAD = 128
F32 = jnp.float32
BF16 = jnp.bfloat16

NT = (((1,), (1,)), ((), ()))
NN = (((1,), (0,)), ((), ()))
TN = (((0,), (0,)), ((), ()))


def mm(a, b, dims):
    return lax.dot_general(a, b, dims, preferred_element_type=F32)


VMEM = pl.BlockSpec(memory_space=pltpu.VMEM)
SMEM = pl.BlockSpec(memory_space=pltpu.SMEM)

def room(mib):
    return pltpu.CompilerParams(vmem_limit_bytes=mib * 1024 * 1024)


COST = pl.CostEstimate(flops=1024, bytes_accessed=1024, transcendentals=0)


def whole_call(body, outs, args, scratch=(), scalars=1, extra=6, away=0):
    inside = len(args) - scalars - away
    held = sum(
        math.prod(a.shape) * a.dtype.itemsize
        for a in (*args[: scalars + inside], *scratch)
        if a.dtype in (F32, BF16)
    ) + sum(math.prod(s) * jnp.dtype(t).itemsize for s, t in outs)
    return pl.pallas_call(
        body,
        out_shape=[jax.ShapeDtypeStruct(s, t) for s, t in outs],
        in_specs=[SMEM] * scalars
        + [VMEM] * inside
        + [pl.BlockSpec(memory_space=pltpu.HBM)] * away,
        out_specs=[VMEM] * len(outs),
        scratch_shapes=list(scratch),
        compiler_params=room(held // 2**20 + extra),
        cost_estimate=COST,
    )(*args)


def to_col(v, k):
    return lax.ppermute(v, "col", [(i, i ^ k) for i in range(4)])


def to_row(v):
    return lax.ppermute(v, "row", [(0, 1), (1, 0)])


def gather_col(v):
    half = v.shape[0] // 2
    a = to_col(v, 1)
    b = to_col(v, 2)
    d = jnp.concatenate([to_col(a[:half], 2), to_col(b[half:], 1)], axis=0)
    return [v, a, b, d]


def exchange_col(parts):
    return [parts[0]] + [to_col(parts[k], k) for k in range(1, 4)]


def after(values, *gates):
    tied = lax.optimization_barrier((values, gates))
    return tied[0]


def sum_dp(v):
    n = lax.axis_size("dp")
    if n == 4:
        return v + sum(
            lax.ppermute(v, "dp", [(i, i ^ k) for i in range(4)]) for k in (1, 2, 3)
        )
    return lax.psum(v, "dp")


def scatter_dp(v):
    if lax.axis_size("dp") != 4:
        return lax.psum_scatter(v, "dp", scatter_dimension=0).astype(F32)
    here = lax.axis_index("dp")
    piece = lambda k: lax.dynamic_index_in_dim(v, here ^ k, 0, keepdims=False)
    total = piece(0).astype(F32)
    for k in (1, 2, 3):
        total = total + lax.ppermute(piece(k), "dp", [(i, i ^ k) for i in range(4)]).astype(F32)
    return total


def natural(parts, here):
    stacked = jnp.stack(parts) if isinstance(parts, list) else parts
    return [lax.dynamic_index_in_dim(stacked, here ^ j, 0, keepdims=False) for j in range(4)]


def half_mask(shape):
    return lax.broadcasted_iota(jnp.int32, shape, len(shape) - 1) % LANES < 64


def swap_halves(v):
    lane = lax.broadcasted_iota(jnp.int32, v.shape, 1) % 64
    return jnp.where(lane < 32, pltpu.roll(v, LANES - 32, 1), pltpu.roll(v, 32, 1))


def rope_of(table):
    first = lax.broadcasted_iota(jnp.int32, table.shape, 1) % 64 < 32
    cos_part = jnp.where(first, table, pltpu.roll(table, 32, 1))
    sin_part = jnp.where(first, -pltpu.roll(table, LANES - 32, 1), table)
    return cos_part, sin_part


def moments(parts, features):
    average = sum(jnp.sum(v, axis=1, keepdims=True) for v in parts) / features
    centered = [v - average for v in parts]
    variance = sum(jnp.sum(v * v, axis=1, keepdims=True) for v in centered) / features
    inverse = lax.rsqrt(variance + NORM_EPSILON)
    return [v * inverse for v in centered], inverse


def lanes_of(ref, rows, p):
    return ref[rows, pl.ds(p * 256, 256)]


def project(low, w_own, table, out):
    cos_part, sin_part = rope_of(table[...])
    got = sum(mm(low[k], w_own[k, :384], NT) for k in range(4))
    query, key, value = got[:, :128], got[:, 128:256], got[:, 256:]
    query = (query * cos_part + swap_halves(query) * sin_part).astype(BF16)
    out[:, :128] = query * jnp.asarray(0.125, BF16)
    out[:, 128:256] = (key * cos_part + swap_halves(key) * sin_part).astype(BF16)
    out[:, 256:] = value.astype(BF16)


def qkv_kernel(
    index, x0, x1, x2, x3a, x3b, gains, w_own, table, own_out, h_out, inv_out, slot_out, x3
):
    step = pl.program_id(0)
    halves = pl.num_programs(0) // 2

    @pl.when(step < halves)
    def _():
        x3[...] = x3a[...]

    @pl.when(step >= halves)
    def _():
        x3[...] = x3b[...]

    refs = (x0, x1, x2, x3)

    @pl.when(step == index[0])
    def _():
        for k, ref in enumerate(refs):
            slot_out[:, k * 256 : (k + 1) * 256] = ref[...]

    parts = [ref[...].astype(F32) for ref in refs]
    units, inverse = moments(parts, 4 * 256)
    inv_out[...] = jnp.broadcast_to(inverse, inv_out.shape)
    low = [(units[k] * gains[k, 0:1, :]).astype(BF16) for k in range(4)]
    for k in range(4):
        h_out[:, k * 256 : (k + 1) * 256] = low[k]
    project(low, w_own, table, own_out)


def away_kernel(index, h, w_own, table, out):
    low = [h[:, k * 256 : (k + 1) * 256] for k in range(4)]
    project(low, w_own, table, out)


def run_qkv(index, xs, gains, w_own, table):
    rows = xs[0].shape[0]
    step = 256
    last = rows // step // 2 - 1
    whole = lambda shape: pl.BlockSpec(shape, lambda i, s: (0,) * len(shape))
    block = lambda n: pl.BlockSpec((step, n), lambda i, s: (i, 0))
    shape = lambda n, t=BF16: jax.ShapeDtypeStruct((rows, n), t)
    return pl.pallas_call(
        qkv_kernel,
        grid_spec=pltpu.PrefetchScalarGridSpec(
            num_scalar_prefetch=1,
            grid=(rows // step,),
            in_specs=[block(256)] * 3
            + [
                pl.BlockSpec((step, 256), lambda i, s: (jnp.minimum(i, last), 0)),
                pl.BlockSpec((step, 256), lambda i, s: (jnp.maximum(i - last - 1, 0), 0)),
            ]
            + [
                whole(gains.shape),
                whole(w_own.shape),
                pl.BlockSpec((step, 128), lambda i, s: (s[1] * (rows // step) + i, 0)),
            ],
            out_specs=[block(384), block(1024), block(128), whole((step, 1024))],
            scratch_shapes=[pltpu.VMEM((step, 256), BF16)],
        ),
        out_shape=[
            shape(384), shape(1024), shape(128, F32), jax.ShapeDtypeStruct((step, 1024), BF16),
        ],
        compiler_params=room(20),
        cost_estimate=COST,
    )(index, *xs, gains, w_own, table)


def run_away(index, h, w_own, table):
    rows = h.shape[0]
    block = lambda n: pl.BlockSpec((256, n), lambda i, s: (i, 0))
    return pl.pallas_call(
        away_kernel,
        grid_spec=pltpu.PrefetchScalarGridSpec(
            num_scalar_prefetch=1,
            grid=(rows // 256,),
            in_specs=[
                block(1024),
                pl.BlockSpec(w_own.shape, lambda i, s: (0, 0, 0)),
                pl.BlockSpec((256, 128), lambda i, s: ((1 - s[1]) * (rows // 256) + i, 0)),
            ],
            out_specs=block(384),
        ),
        out_shape=jax.ShapeDtypeStruct((rows, 384), BF16),
        compiler_params=room(16),
        cost_estimate=COST,
    )(index, h, w_own, table)


def to_columns(row):
    return jnp.transpose(jnp.broadcast_to(row, (LANES, row.shape[1])))


def attend_kernel(info, seg, own, recv, own_out, oth_out, lse_out, qkv, mixed, seg_col, sems):
    length = qkv.shape[0]
    rows = length // 2
    blocks = length // BLOCK
    here = info[4, 0]
    mine = pl.ds(pl.multiple_of(here * rows, rows), rows)
    other = pl.ds(pl.multiple_of((1 - here) * rows, rows), rows)
    copies = [
        pltpu.make_async_copy(own, qkv.at[mine, :], sems.at[0]),
        pltpu.make_async_copy(recv, qkv.at[other, :], sems.at[1]),
    ]
    for copy in copies:
        copy.start()
    for i in range(blocks):
        seg_col[i * BLOCK : (i + 1) * BLOCK, :] = to_columns(seg[:, i * BLOCK : (i + 1) * BLOCK])
    for copy in copies:
        copy.wait()
    low_half = half_mask((BLOCK, LANES))
    zero = jnp.zeros((BLOCK, LANES), BF16)

    def wide_block(at, first, count):
        query = qkv[pl.ds(at, BLOCK), :128]
        pair = jnp.concatenate(
            [jnp.where(low_half, query, zero), jnp.where(low_half, zero, query)], axis=0
        )
        k_at = pl.multiple_of(jnp.minimum(first, blocks - count) * BLOCK, BLOCK)
        span = pl.ds(k_at, count * BLOCK)
        got = mm(pair, qkv[span, 128:256], NT)
        seg_q = seg_col[pl.ds(at, BLOCK), :]
        seg_k = seg[:, span]
        chunks = []
        for j in range(count * 2):
            lanes = slice(j * LANES, (j + 1) * LANES)
            same = seg_q == seg_k[:, lanes]
            chunks.append(
                [
                    jnp.where(same, got[:BLOCK, lanes], MASKED),
                    jnp.where(same, got[BLOCK:, lanes], MASKED),
                ]
            )
        mixing, lse = [], []
        weights = []
        for head in range(2):
            highest = chunks[0][head]
            for j in range(1, count * 2):
                highest = jnp.maximum(highest, chunks[j][head])
            highest = jnp.max(highest, axis=1, keepdims=True)
            weight = [jnp.exp(chunks[j][head] - highest) for j in range(count * 2)]
            total = weight[0]
            for j in range(1, count * 2):
                total = total + weight[j]
            total = jnp.sum(total, axis=1, keepdims=True)
            weights.append(jnp.concatenate([w.astype(BF16) for w in weight], axis=1))
            mixing.append(total)
            lse.append(highest + jnp.log(total))
        both = mm(jnp.concatenate(weights, axis=0), qkv[span, 256:], NN)
        mixed[pl.ds(at, BLOCK), :] = jnp.where(
            low_half, both[:BLOCK] / mixing[0], both[BLOCK:] / mixing[1]
        ).astype(BF16)
        for head in range(2):
            lse_out[head : head + 1, pl.ds(at, BLOCK)] = to_row_form(lse[head])

    def one_block(qb, _):
        at = pl.multiple_of(qb * BLOCK, BLOCK)
        first = info[0, qb]
        need = info[1, qb] - first
        sizes = SIZES
        for i, count in enumerate(sizes):
            least = sizes[i - 1] if i else 0

            @pl.when((need > least) & (need <= count))
            def _(count=count):
                wide_block(at, first, count)

        return 0

    lax.fori_loop(0, blocks, one_block, 0)
    own_out[...] = mixed[pl.ds(pl.multiple_of(here * rows, rows), rows), :]
    oth_out[...] = mixed[pl.ds(pl.multiple_of((1 - here) * rows, rows), rows), :]


def attend_back_kernel(
    info, seg, lse, dm_own, dm_recv, mix_own, mix_oth, own, recv, table_from,
    own_out, oth_out, qkv, dmix, dsum, dquery, dout, seg_col, table, mixed, sems,
):
    length = qkv.shape[0]
    rows = length // 2
    here = info[4, 0]
    mine = pl.ds(pl.multiple_of(here * rows, rows), rows)
    other = pl.ds(pl.multiple_of((1 - here) * rows, rows), rows)
    early = [
        pltpu.make_async_copy(mix_own, mixed.at[mine, :], sems.at[3]),
        pltpu.make_async_copy(mix_oth, mixed.at[other, :], sems.at[4]),
    ]
    copies = [
        pltpu.make_async_copy(own, qkv.at[mine, :], sems.at[0]),
        pltpu.make_async_copy(recv, qkv.at[other, :], sems.at[1]),
        pltpu.make_async_copy(table_from, table, sems.at[2]),
    ]
    for copy in early + copies:
        copy.start()
    dmix[mine, :] = dm_own[...]
    dmix[other, :] = dm_recv[...]
    blocks = length // BLOCK
    for i in range(blocks):
        seg_col[i * BLOCK : (i + 1) * BLOCK, :] = to_columns(seg[:, i * BLOCK : (i + 1) * BLOCK])

    for copy in early:
        copy.wait()

    def inner(qb, _):
        at = pl.multiple_of(qb * BLOCK, BLOCK)
        block = pl.ds(at, BLOCK)
        product = jnp.transpose(dmix[block, :].astype(F32) * mixed[block, :].astype(F32))
        dsum[0:1, pl.ds(at, BLOCK)] = jnp.sum(product[:64], axis=0, keepdims=True)
        dsum[1:2, pl.ds(at, BLOCK)] = jnp.sum(product[64:], axis=0, keepdims=True)
        dquery[pl.ds(at, BLOCK), :] = jnp.zeros((BLOCK, LANES), F32)
        return 0

    lax.fori_loop(0, blocks, inner, 0)
    for copy in copies:
        copy.wait()
    low_half = half_mask((BLOCK, LANES))
    zero = jnp.zeros((BLOCK, LANES), BF16)

    def both(v):
        return jnp.concatenate([jnp.where(low_half, v, zero), jnp.where(low_half, zero, v)], axis=0)

    def wide_block(k_at, first, count):
        key_pair = both(qkv[pl.ds(k_at, BLOCK), 128:256])
        value_pair = both(qkv[pl.ds(k_at, BLOCK), 256:])
        seg_k = seg_col[pl.ds(k_at, BLOCK), :]
        at = pl.multiple_of(jnp.minimum(first, blocks - count) * BLOCK, BLOCK)
        span = pl.ds(at, count * BLOCK)
        query, grad = qkv[span, :128], dmix[span, :]
        got = mm(key_pair, query, NT)
        dgot = mm(value_pair, grad, NT)
        lse_q, dsum_q, seg_q = lse[:, span], dsum[:, span], seg[:, span]
        weights, dscores = [], []
        for head in range(2):
            rows_h = slice(head * BLOCK, (head + 1) * BLOCK)
            weight_h, dscore_h = [], []
            for j in range(count * 2):
                lanes = slice(j * LANES, (j + 1) * LANES)
                same = seg_k == seg_q[:, lanes]
                weight = jnp.exp(
                    jnp.where(same, got[rows_h, lanes] - lse_q[head : head + 1, lanes], MASKED)
                )
                weight_h.append(weight.astype(BF16))
                dscore_h.append(
                    (weight * (dgot[rows_h, lanes] - dsum_q[head : head + 1, lanes])).astype(BF16)
                )
            weights.append(jnp.concatenate(weight_h, axis=1))
            dscores.append(jnp.concatenate(dscore_h, axis=1))
        weights = jnp.concatenate(weights, axis=0)
        dscores = jnp.concatenate(dscores, axis=0)
        dvalue = mm(weights, grad, NN)
        dkey = mm(dscores, query, NN)
        dquery[span, :] += jnp.transpose(mm(key_pair, dscores, TN))
        dkey = jnp.where(low_half, dkey[:BLOCK], dkey[BLOCK:])
        dvalue = jnp.where(low_half, dvalue[:BLOCK], dvalue[BLOCK:])
        cos_part, sin_part = rope_of(table[pl.ds(k_at, BLOCK), :])
        dkey = dkey * cos_part - swap_halves(dkey) * sin_part
        dout[pl.ds(k_at, BLOCK), 128:256] = dkey.astype(BF16)
        dout[pl.ds(k_at, BLOCK), 256:] = dvalue.astype(BF16)

    def one_block(kb, _):
        k_at = pl.multiple_of(kb * BLOCK, BLOCK)
        first = info[0, kb]
        need = info[1, kb] - first
        for i, count in enumerate(SIZES):
            least = SIZES[i - 1] if i else 0

            @pl.when((need > least) & (need <= count))
            def _(count=count):
                wide_block(k_at, first, count)

        return 0

    lax.fori_loop(0, blocks, one_block, 0)

    def finish(qb, _):
        at = pl.multiple_of(qb * BLOCK, BLOCK)
        cos_part, sin_part = rope_of(table[pl.ds(at, BLOCK), :])
        grad = dquery[pl.ds(at, BLOCK), :] * 0.125
        grad = grad * cos_part - swap_halves(grad) * sin_part
        dout[pl.ds(at, BLOCK), :128] = grad.astype(BF16)
        return 0

    lax.fori_loop(0, blocks, finish, 0)
    own_out[...] = dout[mine, :]
    oth_out[...] = dout[other, :]


def run_attend(info, own, recv, seg_row):
    rows, length = own.shape[0], seg_row.shape[1]
    return whole_call(
        attend_kernel,
        [((rows, LANES), BF16), ((rows, LANES), BF16), ((2, length), F32)],
        (info, seg_row, own, recv),
        [
            pltpu.VMEM((length, 384), BF16),
            pltpu.VMEM((length, LANES), BF16),
            pltpu.VMEM((length, LANES), F32),
            pltpu.SemaphoreType.DMA((2,)),
        ],
        away=2,
        extra=46,
    )


def run_attend_back(
    info, own, recv, seg_row, lse, mix_own, mix_away, dm_own, dm_recv, table
):
    rows, length = own.shape[0], seg_row.shape[1]
    return whole_call(
        attend_back_kernel,
        [((rows, 384), BF16), ((rows, 384), BF16)],
        (info, seg_row, lse, dm_own, dm_recv, mix_own, mix_away, own, recv, table),
        [
            pltpu.VMEM((length, 384), BF16),
            pltpu.VMEM((length, LANES), BF16),
            pltpu.VMEM((2, length), F32),
            pltpu.VMEM((length, LANES), F32),
            pltpu.VMEM((length, 384), BF16),
            pltpu.VMEM((length, LANES), F32),
            pltpu.VMEM((length, LANES), F32),
            pltpu.VMEM((length, LANES), BF16),
            pltpu.SemaphoreType.DMA((5,)),
        ],
        extra=36,
        away=5,
    )


def slot_rows(info, k):
    return pl.ds(pl.multiple_of((info[4, 1] ^ k) * 256, 256), 256)


def attn_out_kernel(plan, info, mix_own, mix_oth, w_own, w_oth, *outs):
    for out, pieces in zip(outs, plan):
        at = 0
        for k, first, count in pieces:
            start = pl.multiple_of((info[4, 1] ^ k) * 256 + first, 128)
            rows = pl.ds(start, count)
            mix = jnp.concatenate([mix_own[rows, :], mix_oth[rows, :]], axis=1)
            for p in range(4):
                weight = jnp.concatenate([w_own[k ^ p, 384:512], w_oth[k ^ p, 384:512]], axis=0)
                out[at : at + count, p * 256 : (p + 1) * 256] = mm(mix, weight, NN).astype(BF16)
            at += count


def relay_kernel(first, x, p0, got, part, sent_out, kept_out):
    half = got.shape[0] // 2
    sent_out[...] = (part[...].astype(F32) + got[half:, :].astype(F32)).astype(BF16)
    rows = slice(first, first + half)
    kept_out[...] = x[rows, :].astype(F32) + p0[rows, :].astype(F32) + got[:half, :].astype(F32)


def middle_kernel(kept_a, got_a, kept_b, got_b, out):
    half = kept_a.shape[0]
    out[:half, :] = (kept_a[...] + got_a[...].astype(F32)).astype(BF16)
    out[half:, :] = (kept_b[...] + got_b[...].astype(F32)).astype(BF16)


def ffn_kernel(k, index, *refs):
    pieces = 2 if k == 3 else 1
    part = jnp.concatenate([ref[...] for ref in refs[:pieces]], axis=0)
    d0, d1, d2, d3, gains, w_own, w_oth, *refs = refs[pieces:]
    backs = refs[-pieces:]
    f0, f1, f2, f3, h_out, hid_out, dug_out, mid_out = refs[-8 - pieces : -pieces]
    parts = [part[:, (k ^ p) * 256 : ((k ^ p) + 1) * 256] for p in range(4)]
    mid_out[...] = parts[0]
    units, _ = moments([v.astype(F32) for v in parts], 4 * 256)
    low = [(units[p] * gains[p, 1:2, :]).astype(BF16) for p in range(4)]
    for p in range(4):
        h_out[:, p * 256 : (p + 1) * 256] = low[p]
    grads = [ref[...] for ref in (d0, d1, d2, d3)]

    def weight(p, i):
        rows = slice(i * 384, (i + 1) * 384)
        return jnp.concatenate([w_own[p, rows], w_oth[p, rows]], axis=0)

    gate = sum(mm(low[p], weight(p, 0), NT) for p in range(4))
    up = sum(mm(low[p], weight(p, 1), NT) for p in range(4))
    dhidden = sum(mm(grads[p], weight(p, 2), NT) for p in range(4))
    phi = 0.5 * (1.0 + lax.erf(gate * (2.0**-0.5)))
    density = jnp.exp(-0.5 * gate * gate) * ((2.0 * math.pi) ** -0.5)
    act = gate * phi
    hidden = (act * up).astype(BF16)
    dgate = (dhidden * up * (phi + gate * density)).astype(BF16)
    dup = (dhidden * act).astype(BF16)
    hid_out[...] = hidden
    dug_out[:, :384] = dgate[:, :384]
    dug_out[:, 384:768] = dup[:, :384]
    dug_out[:, 768:1152] = dgate[:, 384:]
    dug_out[:, 1152:] = dup[:, 384:]
    for p in range(4):
        got = mm(dgate, weight(p, 0), NN) + mm(dup, weight(p, 1), NN)
        got = got.astype(BF16)
        for i, out in enumerate(backs):
            out[:, (k ^ p) * 256 : ((k ^ p) + 1) * 256] = got[i * (256 // pieces) : (i + 1) * (256 // pieces)]
    for p, out in enumerate((f0, f1, f2, f3)):
        out[...] = mm(hidden, weight(p, 2), NN).astype(BF16)


def run_ffn(k, index, mids, grads, gains, w_own, w_oth, held):
    rows = grads[0].shape[0]
    whole = lambda shape: pl.BlockSpec(shape, lambda i, s: (0,) * len(shape))
    block = lambda n: pl.BlockSpec((256, n), lambda i, s: (s[0] ^ k, 0))
    widths = [256] * 4 + [1024, 768, 1536, 256]
    outs = pl.pallas_call(
        functools.partial(ffn_kernel, k),
        grid_spec=pltpu.PrefetchScalarGridSpec(
            num_scalar_prefetch=1,
            grid=(1,),
            in_specs=[whole(v.shape) for v in mids]
            + [block(256)] * 4
            + [whole(gains.shape), whole(w_own.shape), whole(w_oth.shape)]
            + [pl.BlockSpec(memory_space=pl.ANY)] * len(held),
            out_specs=[block(n) for n in widths] + [whole(v.shape) for v in mids],
        ),
        out_shape=[jax.ShapeDtypeStruct((rows, n), BF16) for n in widths]
        + [jax.ShapeDtypeStruct(v.shape, BF16) for v in mids],
        input_output_aliases={8 + len(mids) + i: i for i in range(len(held))},
        compiler_params=room(26),
        cost_estimate=COST,
    )(index, *mids, *grads, gains, w_own, w_oth, *held)
    return outs[:8], list(outs[8:])


def pack_kernel(*refs):
    out = refs[-1]
    planes, _, rows, _ = out.shape
    for p in range(4):
        block = slice(p * 256, (p + 1) * 256)
        total = sum(ref[block, :].astype(F32) for ref in refs[:-1]).astype(BF16)
        for d in range(planes):
            out[d, p] = total[d * rows : (d + 1) * rows]


def pack_dp(*terms):
    planes, width = lax.axis_size("dp"), terms[0].shape[1]
    if planes > 16:
        total = sum(v.astype(F32) for v in terms).astype(BF16)
        return jnp.swapaxes(total.reshape(4, planes, 256 // planes, width), 0, 1)
    return whole_call(
        pack_kernel, [((planes, 4, 256 // planes, width), BF16)], terms, scalars=0
    )[0]


def norm_back(grads, units, inverse, gains):
    scaled = [g * w for g, w in zip(grads, gains)]
    first = sum(jnp.sum(v, axis=1, keepdims=True) for v in scaled) / 1024
    second = sum(jnp.sum(v * u, axis=1, keepdims=True) for v, u in zip(scaled, units)) / 1024
    return [inverse * (v - first - u * second) for v, u in zip(scaled, units)]


def middle_back_kernel(info, mid, p0, p1, p2, p3a, p3b, d0, d1, d2, d3, gains, dx_out, dz_out, gain_out):
    rows = slot_rows(info, 0)
    at = [slice(p * 256, (p + 1) * 256) for p in range(4)]
    units, inverse = moments([mid[:, a].astype(F32) for a in at], 1024)
    last = jnp.concatenate([p3a[...], p3b[...]], axis=0)
    grads = [sum(part[:, a].astype(F32) for part in (p0, p1, p2, last)) for a in at]
    back = norm_back(grads, units, inverse, [gains[p, 1:2, :] for p in range(4)])
    for p, dy in enumerate((d0, d1, d2, d3)):
        total = back[p] + dy[rows, :].astype(F32)
        dx_out[:, at[p]] = total
        dz_out[:, at[p]] = total.astype(BF16)
        gain_out[p : p + 1, :] = jnp.sum(grads[p] * units[p], axis=0, keepdims=True)


def mixed_back_kernel(k, index, *refs):
    pieces = 2 if k == 3 else 1
    part = jnp.concatenate([ref[...] for ref in refs[:pieces]], axis=0)
    w_own, w_oth = refs[pieces : pieces + 2]
    own_out, oth_out, dz_out = refs[-3:]
    total = None
    for p in range(4):
        piece = part[:, (k ^ p) * 256 : ((k ^ p) + 1) * 256]
        dz_out[:, p * 256 : (p + 1) * 256] = piece
        term = mm(piece, jnp.concatenate([w_own[p], w_oth[p]], axis=0), NT)
        total = term if total is None else total + term
    own_out[...] = total[:, :128].astype(BF16)
    oth_out[...] = total[:, 128:].astype(BF16)


def run_mixed_back(k, index, parts, w_own, w_oth, held):
    rows = 4 * 256
    whole = lambda shape: pl.BlockSpec(shape, lambda i, s: (0,) * len(shape))
    block = lambda n: pl.BlockSpec((256, n), lambda i, s: (s[0] ^ k, 0))
    weight = pl.BlockSpec((4, 128, 256), lambda i, s: (0, 3, 0))
    return pl.pallas_call(
        functools.partial(mixed_back_kernel, k),
        grid_spec=pltpu.PrefetchScalarGridSpec(
            num_scalar_prefetch=1,
            grid=(1,),
            in_specs=[whole(v.shape) for v in parts]
            + [weight, weight]
            + [pl.BlockSpec(memory_space=pl.ANY)] * len(held),
            out_specs=[block(128), block(128), block(1024)],
        ),
        out_shape=[jax.ShapeDtypeStruct((rows, n), BF16) for n in (128, 128, 1024)],
        input_output_aliases={3 + len(parts) + i: i for i in range(len(held))},
        compiler_params=room(12),
        cost_estimate=COST,
    )(index, *parts, w_own, w_oth, *held)


def to_row_form(column):
    return jnp.transpose(jnp.broadcast_to(column, (column.shape[0], LANES)))[0:1, :]


def input_back_kernel(d_own, d_oth, w_own, w_oth, h, gains, o0, o1, o2, o3, sums_out, gain_out):
    step = pl.program_id(0)
    grad = jnp.concatenate([d_own[...], d_oth[...]], axis=1)
    first = second = None
    for p, out in enumerate((o0, o1, o2, o3)):
        weight = jnp.concatenate([w_own[p, :384], w_oth[p, :384]], axis=0)
        got = mm(grad, weight, NN)
        out[...] = got.astype(BF16)
        crossed = got * h[:, p * 256 : (p + 1) * 256].astype(F32)
        scaled = got * gains[p, 0:1, :]
        scaled = scaled[:, :128] + scaled[:, 128:]
        across = crossed[:, :128] + crossed[:, 128:]
        first = scaled if first is None else first + scaled
        second = across if second is None else second + across
        part = jnp.sum(crossed, axis=0, keepdims=True) / gains[p, 0:1, :]

        @pl.when(step == 0)
        def _():
            gain_out[p : p + 1, :] = part

        @pl.when(step > 0)
        def _():
            gain_out[p : p + 1, :] += part

    sums_out[0:1, :] = jnp.sum(jnp.transpose(first), axis=0, keepdims=True)
    sums_out[1:2, :] = jnp.sum(jnp.transpose(second), axis=0, keepdims=True)


def run_input_back(d_own, d_oth, w_own, w_oth, h, gains):
    rows = h.shape[0]
    whole = lambda shape: pl.BlockSpec(shape, lambda i: (0,) * len(shape))
    block = lambda n: pl.BlockSpec((256, n), lambda i: (i, 0))
    return pl.pallas_call(
        input_back_kernel,
        grid=(rows // 256,),
        in_specs=[block(384), block(384), whole(w_own.shape), whole(w_oth.shape), block(1024), whole(gains.shape)],
        out_specs=[block(256)] * 4 + [pl.BlockSpec((2, 256), lambda i: (0, i)), whole((4, 256))],
        out_shape=[jax.ShapeDtypeStruct((rows, 256), BF16)] * 4
        + [jax.ShapeDtypeStruct((2, rows), F32), jax.ShapeDtypeStruct((4, 256), F32)],
        compiler_params=room(24),
        cost_estimate=COST,
    )(d_own, d_oth, w_own, w_oth, h, gains)


def input_grad_kernel(p0, p1, p2, p3, sums, h, dz, inv, gains, out):
    first = to_columns(sums[0:1, :]) / 1024
    second = to_columns(sums[1:2, :]) / 1024
    both = lambda v: jnp.concatenate([v, v], axis=1)
    gain = gains[0, 0:1, :]
    total = sum(ref[...].astype(F32) for ref in (p0, p1, p2, p3)) * gain
    unit = h[...].astype(F32) / gain
    out[...] = dz[...].astype(F32) + both(inv[...]) * (total - both(first) - unit * both(second))


def run_input_grad(parts, sums, h, dz, inv, gains):
    rows = h.shape[0]
    block = lambda n: pl.BlockSpec((256, n), lambda i: (i, 0))
    return pl.pallas_call(
        input_grad_kernel,
        grid=(rows // 256,),
        in_specs=[block(256)] * 4
        + [pl.BlockSpec((2, 256), lambda i: (0, i)), block(256), block(256), block(128)]
        + [pl.BlockSpec(gains.shape, lambda i: (0, 0, 0))],
        out_specs=block(256),
        out_shape=jax.ShapeDtypeStruct((rows, 256), F32),
        compiler_params=room(12),
        cost_estimate=COST,
    )(*parts, sums, h, dz, inv, gains)


def adam_update(master, first_moment, second, gradient, factor, decay_rate, step_rate):
    scaled = gradient * factor
    first_new = BETA_ONE * first_moment + (1.0 - BETA_ONE) * scaled
    second_new = BETA_TWO * second + (1.0 - BETA_TWO) * scaled * scaled
    first_hat = first_new / (1.0 - BETA_ONE**STEP)
    second_hat = second_new / (1.0 - BETA_TWO**STEP)
    master_new = master - step_rate * (
        first_hat / (jnp.sqrt(second_hat) + ADAM_EPSILON) + decay_rate * master
    )
    return (first_new, second_new, master_new)


def positions(segment):
    length = segment.shape[0]
    number = jnp.arange(length, dtype=jnp.int32)
    before = jnp.concatenate([segment[:1] - 1, segment[:-1]])
    change_marks = jnp.where(segment != before, number, jnp.zeros_like(number))
    return number - lax.cummax(change_marks, axis=0)


def rope_table(place):
    lane = jnp.arange(LANES) % 64
    frequency = ROPE_BASE ** (-(2.0 * (lane % 32).astype(F32)) / 64)
    turned = place.astype(F32)[:, None] * frequency[None, :]
    return jnp.where(lane[None, :] < 32, jnp.cos(turned), jnp.sin(turned))


def on_device(
    tokens, segment_ids, cotangent, qkv_weight, attn_weight, in_weight, out_weight, norm_gains,
    qkv_master, attn_master, in_master, out_master,
    qkv_first, attn_first, in_first, out_first,
    qkv_second, attn_second, in_second, out_second,
    gains_first, gains_second,
):
    col, row = lax.axis_index("col"), lax.axis_index("row")
    segment = segment_ids[0]
    length = segment.shape[0]
    rows = length // 2
    blocks = length // BLOCK
    ff_here = in_weight.shape[2] // 4
    ff_pad = -ff_here % FF_PAD
    ff_wide = ff_here + ff_pad

    qkv_t = jnp.transpose(qkv_weight, (1, 2, 3, 0))
    attn_t = attn_weight.reshape(4, LANES, 256)
    in_t = jnp.transpose(in_weight, (1, 2, 0)).reshape(2, 4, ff_here, 256)
    out_t = out_weight.reshape(4, ff_here, 256)

    index = jnp.stack([col, row])
    a = to_col(tokens, 1)
    b = to_col(tokens, 2)
    high = norm_gains.astype(BF16)
    rest = norm_gains - high.astype(F32)
    middle = rest.astype(BF16)
    lowest = (rest - middle.astype(F32)).astype(BF16)
    gain_rows = jnp.concatenate([high, middle, lowest, jnp.zeros((10, 256), BF16)], axis=0)
    gain_rows = lax.optimization_barrier(gain_rows)

    def wide_piece(k):
        qkv = lax.dynamic_slice_in_dim(qkv_t, 2 * (col ^ k), 2, 1).reshape(3 * LANES, 256)
        return jnp.concatenate(
            [qkv, lax.dynamic_index_in_dim(attn_t, col ^ k, 0, keepdims=False), gain_rows], axis=0
        )

    half = tokens.shape[0] // 2
    x3a, x3b = to_col(a[:half], 2), to_col(b[half:], 1)
    xs = [tokens, a, b, x3a, x3b]
    wa_parts = exchange_col([wide_piece(k) for k in range(4)])
    wa_own = jnp.stack(after(wa_parts, x3a, x3b))
    ff_gate = (x3a, x3b)
    gains = wa_own[:, 512:518].astype(F32).reshape(4, 3, 2, 256)
    gains = gains[:, 0] + gains[:, 1] + gains[:, 2]

    planes = lax.axis_size("dp")
    fill = [(0, 0), (0, 0), (0, ff_pad), (0, 0)]
    ff_t = jnp.pad(jnp.concatenate([in_t, out_t[None]], axis=0), fill)
    ff_t = ff_t.reshape(3, 4, planes, ff_wide // planes, 256)
    ff_t = lax.dynamic_index_in_dim(ff_t, lax.axis_index("dp"), 2, keepdims=False)
    ff_parts = [lax.dynamic_index_in_dim(ff_t, col ^ k, 1, keepdims=False) for k in range(4)]
    ff_parts = exchange_col(after(ff_parts, *ff_gate))
    first = segment[::BLOCK]
    last = segment[BLOCK - 1 :: BLOCK]
    low = jnp.sum((segment[None, :] < first[:, None]).astype(jnp.int32), axis=1) // BLOCK
    high = (
        jnp.sum((segment[None, :] <= last[:, None]).astype(jnp.int32), axis=1) + BLOCK - 1
    ) // BLOCK
    place_here = jnp.zeros((blocks,), jnp.int32).at[0].set(row).at[1].set(col)
    info = jnp.stack([low, high, first, last, place_here])
    seg_row = segment_ids.astype(F32)
    table = rope_table(positions(segment))
    own, h1, inv, x_slot = run_qkv(index, xs, gains, wa_own, table)
    h1_recv = to_row(h1)
    dys = exchange_col([after(cotangent, own)] * 4)
    wa_oth = to_row(after(wa_own, own))
    ff_own = lax.all_gather(jnp.stack(after(ff_parts, own)), "dp", axis=2)
    recv = run_away(index, h1_recv, wa_own, table)
    mix_own, mix_away, lse = run_attend(info, own, recv, seg_row)
    mix_own, mix_away, lse, dys, wa_oth = after((mix_own, mix_away, lse, dys, wa_oth), wa_oth)
    mix_oth = to_row(mix_away)
    def attn_out(*plan):
        return whole_call(
            functools.partial(attn_out_kernel, plan),
            [((sum(count for _, _, count in pieces), 1024), BF16) for pieces in plan],
            (info, mix_own, mix_oth, wa_own, wa_oth),
        )

    x_first, y_first = attn_out(((1, 0, 128), (3, 0, 128)), ((2, 128, 128), (3, 128, 128)))
    x_first, y_first = to_col(x_first, 1), to_col(y_first, 2)
    x_part, y_part, part = attn_out(((1, 128, 128),), ((2, 0, 128),), ((0, 0, 256),))
    relay = lambda first, got, mine: whole_call(
        functools.partial(relay_kernel, first),
        [((128, 1024), BF16), ((128, 1024), F32)],
        (x_slot, part, got, mine),
        scalars=0,
    )
    y_second, kept_a = relay(0, x_first, y_part)
    x_second, kept_b = relay(128, y_first, x_part)
    y_second, x_second = to_col(y_second, 2), to_col(x_second, 1)
    (middle,) = whole_call(
        middle_kernel, [((256, 1024), BF16)], (kept_a, y_second, kept_b, x_second), scalars=0
    )
    ff_own = after(ff_own, x_second, y_second).reshape(4, 3 * ff_wide, 256)
    ff_oth = to_row(ff_own)
    m1, m2 = to_col(middle, 1), to_col(middle, 2)
    held, backward = (), [None] * 4
    for k in range(4):
        if k == 1:
            r1, r2 = after((m1, m2), held[0])
            m3a, m3b = to_col(r1[:128], 2), to_col(r2[128:], 1)
        mids = ((middle,), (m1,), (m2,), (m3a, m3b))[k] if k else (middle,)
        held, part = run_ffn(k, index, mids, dys, gains, ff_own, ff_oth, held)
        if k == 1:
            part, m2 = after((part, m2), m3a, m3b)
        backward[k] = [to_col(v, k) for v in part] if k else part
    forward = held[:4]
    h2, hidden, dug, mid_here = held[4:]
    dx_mid, dz, gain_two = whole_call(
        middle_back_kernel,
        [((256, 1024), F32), ((256, 1024), BF16), ((4, 256), F32)],
        (info, middle, *sum(backward, []), *dys, gains),
    )
    z1, z2 = to_col(dz, 1), to_col(dz, 2)
    z3a, z3b = to_col(z1[:128], 2), to_col(z2[128:], 1)

    h2, hidden, dug = after((h2, hidden, dug), z1, z2)
    dy_all = jnp.concatenate(dys, axis=1)
    ffn_own, ffn_oth = (
        jnp.concatenate(
            [
                mm(h2, dug[:, i * 2 * ff_wide : (i + 1) * 2 * ff_wide], TN).astype(BF16),
                mm(dy_all, hidden[:, i * ff_wide : (i + 1) * ff_wide], TN).astype(BF16),
            ],
            axis=1,
        )
        for i in range(2)
    )
    ffn_oth = to_row(ffn_oth)
    ffn_oth, z3a, z3b = after((ffn_oth, z3a, z3b), z3a, z3b)
    ffn_grad = lax.psum_scatter(pack_dp(ffn_own, ffn_oth), "dp", scatter_dimension=0).astype(F32)

    held = ()
    for k, parts in enumerate(((dz,), (z1,), (z2,), (z3a, z3b))):
        held = run_mixed_back(k, index, parts, wa_own, wa_oth, held)
    dm_own, dm_away, dz_here = held
    dm_recv = to_row(dm_away)
    forward = exchange_col(after(forward, dm_own))
    dq_own, dq_away = run_attend_back(
        info, own, recv, seg_row, lse, mix_own, mix_away, dm_own, dm_recv, table
    )
    dq_own, dq_away, forward, dz_here = after((dq_own, dq_away, forward, dz_here), forward[1:])
    layer_out = (mid_here.astype(F32) + sum(v.astype(F32) for v in forward)).astype(BF16)
    dq_oth = to_row(dq_away)

    attn_both = mm(dz_here, jnp.concatenate([mix_own, mix_oth], axis=1), TN)
    attn_sent = to_row(attn_both[:, LANES:].astype(BF16))
    attn_sum = (attn_both[:, :LANES] + attn_sent.astype(F32)).astype(BF16)
    qkv_sum = (mm(h1, dq_own, TN) + mm(h1_recv, dq_away, TN)).astype(BF16)

    *partial_first, sums, gain_one = run_input_back(dq_own, dq_oth, wa_own, wa_oth, h1, gains)
    notes = [
        jnp.concatenate([sums, jnp.pad(jnp.stack([gain_one[k], gain_two[k]]), [(0, 0), (0, rows - 256)])])
        for k in range(4)
    ]
    late = after(pack_dp(jnp.concatenate([qkv_sum, attn_sum], axis=1)), gain_one)
    late = scatter_dp(late)
    notes = exchange_col(notes)
    partial_first = exchange_col(after(partial_first, notes[1]))
    note = sum(notes)
    input_grad = run_input_grad(partial_first, note[:2], h1, dz_here, inv, gains)

    early = ffn_grad.astype(BF16)
    early = natural(exchange_col([early[k] for k in range(4)]), col)
    late = after(late, *partial_first[1:])
    squares = jnp.sum(ffn_grad * ffn_grad) + jnp.sum(late * late)
    message = jnp.concatenate([note[2:, :256], jnp.full((6, 256), squares)], axis=0)
    message = sum_dp(message)
    message = message + to_row(message)
    gain_grad = message[:2]
    total = message[2:3, :LANES] + jnp.sum(gain_grad * gain_grad)
    total = jnp.broadcast_to(total, (8, LANES))
    total, early = after((total, early), *early)
    total = sum(exchange_col([total] * 4))
    grad_norm = jnp.sqrt(total[0, 0])
    factor = CLIP_NORM / (grad_norm + 1e-06)

    shard = late.shape[1]
    late = late.astype(BF16)
    late = natural(exchange_col([late[k] for k in range(4)]), col)
    grad_qkv = jnp.stack([v[:, : 3 * LANES].reshape(shard, 3, 2, 64) for v in late], axis=2).reshape(
        qkv_master.shape
    )
    grad_attn = jnp.concatenate([v[:, 3 * LANES :] for v in late], axis=1).T.reshape(
        attn_master.shape
    )
    grad_in = jnp.stack(
        [
            jnp.concatenate([v[:, i * ff_wide : i * ff_wide + ff_here] for v in early], axis=1)
            for i in range(2)
        ],
        axis=1,
    )
    grad_out = jnp.concatenate([v[:, 2 * ff_wide : 2 * ff_wide + ff_here] for v in early], axis=1).T

    grad_qkv, grad_attn, grad_in, grad_out = (
        v.astype(F32) for v in (grad_qkv, grad_attn, grad_in, grad_out)
    )
    qkv_new = adam_update(
        qkv_master, qkv_first, qkv_second, grad_qkv, factor, WEIGHT_DECAY, LEARN_RATE
    )
    attn_new = adam_update(
        attn_master, attn_first, attn_second, grad_attn, factor, WEIGHT_DECAY, LEARN_RATE
    )
    in_new = adam_update(in_master, in_first, in_second, grad_in, factor, WEIGHT_DECAY, LEARN_RATE)
    out_new = adam_update(
        out_master, out_first, out_second, grad_out, factor, WEIGHT_DECAY, LEARN_RATE
    )
    gains_new = adam_update(
        norm_gains, gains_first, gains_second, gain_grad, factor, 0.0, GAIN_RATE
    )
    return (
        layer_out, input_grad, grad_norm,
        qkv_new[0], attn_new[0], in_new[0], out_new[0],
        qkv_new[1], attn_new[1], in_new[1], out_new[1],
        qkv_new[2], attn_new[2], in_new[2], out_new[2],
        qkv_new[2].astype(BF16), attn_new[2].astype(BF16),
        in_new[2].astype(BF16), out_new[2].astype(BF16),
        gains_new[0], gains_new[1], gains_new[2],
    )


def solution(mesh):
    activations = P(("dp", "row"), "col")
    gains = P(None, "col")
    weights = (
        P("col", None, "row", None), P("row", None, "col"), P("col", None, "row"), P("row", "col"),
    )
    states = (
        P(("col", "dp"), None, "row", None), P("row", None, ("col", "dp")),
        P(("col", "dp"), None, "row"), P("row", ("col", "dp")),
    )
    return jax.shard_map(
        on_device,
        mesh=mesh,
        in_specs=(activations, P("dp", None), activations, *weights, gains)
        + states * 3
        + (gains, gains),
        out_specs=(activations, activations, P()) + states * 4 + (gains, gains, gains),
        check_vma=False,
    )
```

```python
import functools
import math

import jax
import jax.numpy as jnp
from jax import lax
from jax.experimental import pallas as pl
from jax.experimental.pallas import tpu as pltpu
from jax.sharding import PartitionSpec as P

STEP = 10


NORM_EPSILON = 1e-05
ROPE_BASE = 160000.0
CLIP_NORM = 1.0
LEARN_RATE = 0.02
GAIN_RATE = 0.5
BETA_ONE = 0.9
BETA_TWO = 0.98
ADAM_EPSILON = 1e-08
WEIGHT_DECAY = 0.01
MASKED = -1e30
SIZES = (1, 2, 3, 4, 5, 6, 7, 8)

BLOCK = 256
LANES = 128
FF_PAD = 128
F32 = jnp.float32
BF16 = jnp.bfloat16

NT = (((1,), (1,)), ((), ()))
NN = (((1,), (0,)), ((), ()))
TN = (((0,), (0,)), ((), ()))


def mm(a, b, dims):
    return lax.dot_general(a, b, dims, preferred_element_type=F32)


VMEM = pl.BlockSpec(memory_space=pltpu.VMEM)
SMEM = pl.BlockSpec(memory_space=pltpu.SMEM)

def room(mib):
    return pltpu.CompilerParams(vmem_limit_bytes=mib * 1024 * 1024)


COST = pl.CostEstimate(flops=1024, bytes_accessed=1024, transcendentals=0)


def whole_call(body, outs, args, scratch=(), scalars=1, extra=6, away=0):
    inside = len(args) - scalars - away
    held = sum(
        math.prod(a.shape) * a.dtype.itemsize
        for a in (*args[: scalars + inside], *scratch)
        if a.dtype in (F32, BF16)
    ) + sum(math.prod(s) * jnp.dtype(t).itemsize for s, t in outs)
    return pl.pallas_call(
        body,
        out_shape=[jax.ShapeDtypeStruct(s, t) for s, t in outs],
        in_specs=[SMEM] * scalars
        + [VMEM] * inside
        + [pl.BlockSpec(memory_space=pltpu.HBM)] * away,
        out_specs=[VMEM] * len(outs),
        scratch_shapes=list(scratch),
        compiler_params=room(held // 2**20 + extra),
        cost_estimate=COST,
    )(*args)


def to_col(v, k):
    return lax.ppermute(v, "col", [(i, i ^ k) for i in range(4)])


def to_row(v):
    return lax.ppermute(v, "row", [(0, 1), (1, 0)])


def gather_col(v):
    half = v.shape[0] // 2
    a = to_col(v, 1)
    b = to_col(v, 2)
    d = jnp.concatenate([to_col(a[:half], 2), to_col(b[half:], 1)], axis=0)
    return [v, a, b, d]


def exchange_col(parts):
    return [parts[0]] + [to_col(parts[k], k) for k in range(1, 4)]


def after(values, *gates):
    tied = lax.optimization_barrier((values, gates))
    return tied[0]


def sum_dp(v):
    n = lax.axis_size("dp")
    if n == 4:
        return v + sum(
            lax.ppermute(v, "dp", [(i, i ^ k) for i in range(4)]) for k in (1, 2, 3)
        )
    return lax.psum(v, "dp")


def scatter_dp(v):
    if lax.axis_size("dp") != 4:
        return lax.psum_scatter(v, "dp", scatter_dimension=0).astype(F32)
    here = lax.axis_index("dp")
    piece = lambda k: lax.dynamic_index_in_dim(v, here ^ k, 0, keepdims=False)
    total = piece(0).astype(F32)
    for k in (1, 2, 3):
        total = total + lax.ppermute(piece(k), "dp", [(i, i ^ k) for i in range(4)]).astype(F32)
    return total


def natural(parts, here):
    stacked = jnp.stack(parts) if isinstance(parts, list) else parts
    return [lax.dynamic_index_in_dim(stacked, here ^ j, 0, keepdims=False) for j in range(4)]


def half_mask(shape):
    return lax.broadcasted_iota(jnp.int32, shape, len(shape) - 1) % LANES < 64


def swap_halves(v):
    lane = lax.broadcasted_iota(jnp.int32, v.shape, 1) % 64
    return jnp.where(lane < 32, pltpu.roll(v, LANES - 32, 1), pltpu.roll(v, 32, 1))


def rope_of(table):
    first = lax.broadcasted_iota(jnp.int32, table.shape, 1) % 64 < 32
    cos_part = jnp.where(first, table, pltpu.roll(table, 32, 1))
    sin_part = jnp.where(first, -pltpu.roll(table, LANES - 32, 1), table)
    return cos_part, sin_part


def moments(parts, features):
    average = sum(jnp.sum(v, axis=1, keepdims=True) for v in parts) / features
    centered = [v - average for v in parts]
    variance = sum(jnp.sum(v * v, axis=1, keepdims=True) for v in centered) / features
    inverse = lax.rsqrt(variance + NORM_EPSILON)
    return [v * inverse for v in centered], inverse


def lanes_of(ref, rows, p):
    return ref[rows, pl.ds(p * 256, 256)]


def project(low, w_own, table, out):
    cos_part, sin_part = rope_of(table[...])
    got = sum(mm(low[k], w_own[k, :384], NT) for k in range(4))
    query, key, value = got[:, :128], got[:, 128:256], got[:, 256:]
    query = (query * cos_part + swap_halves(query) * sin_part).astype(BF16)
    out[:, :128] = query * jnp.asarray(0.125, BF16)
    out[:, 128:256] = (key * cos_part + swap_halves(key) * sin_part).astype(BF16)
    out[:, 256:] = value.astype(BF16)


def qkv_kernel(
    index, x0, x1, x2, x3a, x3b, gains, w_own, table, own_out, h_out, inv_out, slot_out, x3
):
    step = pl.program_id(0)
    halves = pl.num_programs(0) // 2

    @pl.when(step < halves)
    def _():
        x3[...] = x3a[...]

    @pl.when(step >= halves)
    def _():
        x3[...] = x3b[...]

    refs = (x0, x1, x2, x3)

    @pl.when(step == index[0])
    def _():
        for k, ref in enumerate(refs):
            slot_out[:, k * 256 : (k + 1) * 256] = ref[...]

    parts = [ref[...].astype(F32) for ref in refs]
    units, inverse = moments(parts, 4 * 256)
    inv_out[...] = jnp.broadcast_to(inverse, inv_out.shape)
    low = [(units[k] * gains[k, 0:1, :]).astype(BF16) for k in range(4)]
    for k in range(4):
        h_out[:, k * 256 : (k + 1) * 256] = low[k]
    project(low, w_own, table, own_out)


def away_kernel(index, h, w_own, table, out):
    low = [h[:, k * 256 : (k + 1) * 256] for k in range(4)]
    project(low, w_own, table, out)


def run_qkv(index, xs, gains, w_own, table):
    rows = xs[0].shape[0]
    step = 256
    last = rows // step // 2 - 1
    whole = lambda shape: pl.BlockSpec(shape, lambda i, s: (0,) * len(shape))
    block = lambda n: pl.BlockSpec((step, n), lambda i, s: (i, 0))
    shape = lambda n, t=BF16: jax.ShapeDtypeStruct((rows, n), t)
    return pl.pallas_call(
        qkv_kernel,
        grid_spec=pltpu.PrefetchScalarGridSpec(
            num_scalar_prefetch=1,
            grid=(rows // step,),
            in_specs=[block(256)] * 3
            + [
                pl.BlockSpec((step, 256), lambda i, s: (jnp.minimum(i, last), 0)),
                pl.BlockSpec((step, 256), lambda i, s: (jnp.maximum(i - last - 1, 0), 0)),
            ]
            + [
                whole(gains.shape),
                whole(w_own.shape),
                pl.BlockSpec((step, 128), lambda i, s: (s[1] * (rows // step) + i, 0)),
            ],
            out_specs=[block(384), block(1024), block(128), whole((step, 1024))],
            scratch_shapes=[pltpu.VMEM((step, 256), BF16)],
        ),
        out_shape=[
            shape(384), shape(1024), shape(128, F32), jax.ShapeDtypeStruct((step, 1024), BF16),
        ],
        compiler_params=room(20),
        cost_estimate=COST,
    )(index, *xs, gains, w_own, table)


def run_away(index, h, w_own, table):
    rows = h.shape[0]
    block = lambda n: pl.BlockSpec((512, n), lambda i, s: (i, 0))
    return pl.pallas_call(
        away_kernel,
        grid_spec=pltpu.PrefetchScalarGridSpec(
            num_scalar_prefetch=1,
            grid=(rows // 512,),
            in_specs=[
                block(1024),
                pl.BlockSpec(w_own.shape, lambda i, s: (0, 0, 0)),
                pl.BlockSpec((512, 128), lambda i, s: ((1 - s[1]) * (rows // 512) + i, 0)),
            ],
            out_specs=block(384),
        ),
        out_shape=jax.ShapeDtypeStruct((rows, 384), BF16),
        compiler_params=room(16),
        cost_estimate=COST,
    )(index, h, w_own, table)


def to_columns(row):
    return jnp.transpose(jnp.broadcast_to(row, (LANES, row.shape[1])))


def attend_kernel(info, seg, own, recv, own_out, oth_out, lse_out, qkv, mixed, seg_col, sems):
    length = qkv.shape[0]
    rows = length // 2
    blocks = length // BLOCK
    here = info[4, 0]
    mine = pl.ds(pl.multiple_of(here * rows, rows), rows)
    other = pl.ds(pl.multiple_of((1 - here) * rows, rows), rows)
    copies = [
        pltpu.make_async_copy(own, qkv.at[mine, :], sems.at[0]),
        pltpu.make_async_copy(recv, qkv.at[other, :], sems.at[1]),
    ]
    for copy in copies:
        copy.start()
    for i in range(blocks):
        seg_col[i * BLOCK : (i + 1) * BLOCK, :] = to_columns(seg[:, i * BLOCK : (i + 1) * BLOCK])
    for copy in copies:
        copy.wait()
    low_half = half_mask((BLOCK, LANES))
    zero = jnp.zeros((BLOCK, LANES), BF16)

    def wide_block(at, first, count):
        query = qkv[pl.ds(at, BLOCK), :128]
        pair = jnp.concatenate(
            [jnp.where(low_half, query, zero), jnp.where(low_half, zero, query)], axis=0
        )
        k_at = pl.multiple_of(jnp.minimum(first, blocks - count) * BLOCK, BLOCK)
        span = pl.ds(k_at, count * BLOCK)
        got = mm(pair, qkv[span, 128:256], NT)
        seg_q = seg_col[pl.ds(at, BLOCK), :]
        seg_k = seg[:, span]
        chunks = []
        for j in range(count * 2):
            lanes = slice(j * LANES, (j + 1) * LANES)
            same = seg_q == seg_k[:, lanes]
            chunks.append(
                [
                    jnp.where(same, got[:BLOCK, lanes], MASKED),
                    jnp.where(same, got[BLOCK:, lanes], MASKED),
                ]
            )
        mixing, lse = [], []
        weights = []
        for head in range(2):
            highest = chunks[0][head]
            for j in range(1, count * 2):
                highest = jnp.maximum(highest, chunks[j][head])
            highest = jnp.max(highest, axis=1, keepdims=True)
            weight = [jnp.exp(chunks[j][head] - highest) for j in range(count * 2)]
            total = weight[0]
            for j in range(1, count * 2):
                total = total + weight[j]
            total = jnp.sum(total, axis=1, keepdims=True)
            weights.append(jnp.concatenate([w.astype(BF16) for w in weight], axis=1))
            mixing.append(total)
            lse.append(highest + jnp.log(total))
        both = mm(jnp.concatenate(weights, axis=0), qkv[span, 256:], NN)
        mixed[pl.ds(at, BLOCK), :] = jnp.where(
            low_half, both[:BLOCK] / mixing[0], both[BLOCK:] / mixing[1]
        ).astype(BF16)
        for head in range(2):
            lse_out[head : head + 1, pl.ds(at, BLOCK)] = to_row_form(lse[head])

    def one_block(qb, _):
        at = pl.multiple_of(qb * BLOCK, BLOCK)
        first = info[0, qb]
        need = info[1, qb] - first
        sizes = SIZES
        for i, count in enumerate(sizes):
            least = sizes[i - 1] if i else 0

            @pl.when((need > least) & (need <= count))
            def _(count=count):
                wide_block(at, first, count)

        return 0

    lax.fori_loop(0, blocks, one_block, 0)
    own_out[...] = mixed[pl.ds(pl.multiple_of(here * rows, rows), rows), :]
    oth_out[...] = mixed[pl.ds(pl.multiple_of((1 - here) * rows, rows), rows), :]


def attend_back_kernel(
    info, seg, lse, dm_own, dm_recv, mix_own, mix_oth, own, recv, table_from,
    own_out, oth_out, qkv, dmix, dsum, dquery, dout, seg_col, table, mixed, sems,
):
    length = qkv.shape[0]
    rows = length // 2
    here = info[4, 0]
    mine = pl.ds(pl.multiple_of(here * rows, rows), rows)
    other = pl.ds(pl.multiple_of((1 - here) * rows, rows), rows)
    early = [
        pltpu.make_async_copy(mix_own, mixed.at[mine, :], sems.at[3]),
        pltpu.make_async_copy(mix_oth, mixed.at[other, :], sems.at[4]),
    ]
    copies = [
        pltpu.make_async_copy(own, qkv.at[mine, :], sems.at[0]),
        pltpu.make_async_copy(recv, qkv.at[other, :], sems.at[1]),
        pltpu.make_async_copy(table_from, table, sems.at[2]),
    ]
    for copy in early + copies:
        copy.start()
    dmix[mine, :] = dm_own[...]
    dmix[other, :] = dm_recv[...]
    blocks = length // BLOCK
    for i in range(blocks):
        seg_col[i * BLOCK : (i + 1) * BLOCK, :] = to_columns(seg[:, i * BLOCK : (i + 1) * BLOCK])

    for copy in early:
        copy.wait()

    def inner(qb, _):
        at = pl.multiple_of(qb * BLOCK, BLOCK)
        block = pl.ds(at, BLOCK)
        product = jnp.transpose(dmix[block, :].astype(F32) * mixed[block, :].astype(F32))
        dsum[0:1, pl.ds(at, BLOCK)] = jnp.sum(product[:64], axis=0, keepdims=True)
        dsum[1:2, pl.ds(at, BLOCK)] = jnp.sum(product[64:], axis=0, keepdims=True)
        dquery[pl.ds(at, BLOCK), :] = jnp.zeros((BLOCK, LANES), F32)
        return 0

    lax.fori_loop(0, blocks, inner, 0)
    for copy in copies:
        copy.wait()
    low_half = half_mask((BLOCK, LANES))
    zero = jnp.zeros((BLOCK, LANES), BF16)

    def both(v):
        return jnp.concatenate([jnp.where(low_half, v, zero), jnp.where(low_half, zero, v)], axis=0)

    def wide_block(k_at, first, count):
        key_pair = both(qkv[pl.ds(k_at, BLOCK), 128:256])
        value_pair = both(qkv[pl.ds(k_at, BLOCK), 256:])
        seg_k = seg_col[pl.ds(k_at, BLOCK), :]
        at = pl.multiple_of(jnp.minimum(first, blocks - count) * BLOCK, BLOCK)
        span = pl.ds(at, count * BLOCK)
        query, grad = qkv[span, :128], dmix[span, :]
        got = mm(key_pair, query, NT)
        dgot = mm(value_pair, grad, NT)
        lse_q, dsum_q, seg_q = lse[:, span], dsum[:, span], seg[:, span]
        weights, dscores = [], []
        for head in range(2):
            rows_h = slice(head * BLOCK, (head + 1) * BLOCK)
            weight_h, dscore_h = [], []
            for j in range(count * 2):
                lanes = slice(j * LANES, (j + 1) * LANES)
                same = seg_k == seg_q[:, lanes]
                weight = jnp.exp(
                    jnp.where(same, got[rows_h, lanes] - lse_q[head : head + 1, lanes], MASKED)
                )
                weight_h.append(weight.astype(BF16))
                dscore_h.append(
                    (weight * (dgot[rows_h, lanes] - dsum_q[head : head + 1, lanes])).astype(BF16)
                )
            weights.append(jnp.concatenate(weight_h, axis=1))
            dscores.append(jnp.concatenate(dscore_h, axis=1))
        weights = jnp.concatenate(weights, axis=0)
        dscores = jnp.concatenate(dscores, axis=0)
        dvalue = mm(weights, grad, NN)
        dkey = mm(dscores, query, NN)
        dquery[span, :] += jnp.transpose(mm(key_pair, dscores, TN))
        dkey = jnp.where(low_half, dkey[:BLOCK], dkey[BLOCK:])
        dvalue = jnp.where(low_half, dvalue[:BLOCK], dvalue[BLOCK:])
        cos_part, sin_part = rope_of(table[pl.ds(k_at, BLOCK), :])
        dkey = dkey * cos_part - swap_halves(dkey) * sin_part
        dout[pl.ds(k_at, BLOCK), 128:256] = dkey.astype(BF16)
        dout[pl.ds(k_at, BLOCK), 256:] = dvalue.astype(BF16)

    def one_block(kb, _):
        k_at = pl.multiple_of(kb * BLOCK, BLOCK)
        first = info[0, kb]
        need = info[1, kb] - first
        for i, count in enumerate(SIZES):
            least = SIZES[i - 1] if i else 0

            @pl.when((need > least) & (need <= count))
            def _(count=count):
                wide_block(k_at, first, count)

        return 0

    lax.fori_loop(0, blocks, one_block, 0)

    def finish(qb, _):
        at = pl.multiple_of(qb * BLOCK, BLOCK)
        cos_part, sin_part = rope_of(table[pl.ds(at, BLOCK), :])
        grad = dquery[pl.ds(at, BLOCK), :] * 0.125
        grad = grad * cos_part - swap_halves(grad) * sin_part
        dout[pl.ds(at, BLOCK), :128] = grad.astype(BF16)
        return 0

    lax.fori_loop(0, blocks, finish, 0)
    own_out[...] = dout[mine, :]
    oth_out[...] = dout[other, :]


def run_attend(info, own, recv, seg_row):
    rows, length = own.shape[0], seg_row.shape[1]
    return whole_call(
        attend_kernel,
        [((rows, LANES), BF16), ((rows, LANES), BF16), ((2, length), F32)],
        (info, seg_row, own, recv),
        [
            pltpu.VMEM((length, 384), BF16),
            pltpu.VMEM((length, LANES), BF16),
            pltpu.VMEM((length, LANES), F32),
            pltpu.SemaphoreType.DMA((2,)),
        ],
        away=2,
        extra=46,
    )


def run_attend_back(
    info, own, recv, seg_row, lse, mix_own, mix_away, dm_own, dm_recv, table
):
    rows, length = own.shape[0], seg_row.shape[1]
    return whole_call(
        attend_back_kernel,
        [((rows, 384), BF16), ((rows, 384), BF16)],
        (info, seg_row, lse, dm_own, dm_recv, mix_own, mix_away, own, recv, table),
        [
            pltpu.VMEM((length, 384), BF16),
            pltpu.VMEM((length, LANES), BF16),
            pltpu.VMEM((2, length), F32),
            pltpu.VMEM((length, LANES), F32),
            pltpu.VMEM((length, 384), BF16),
            pltpu.VMEM((length, LANES), F32),
            pltpu.VMEM((length, LANES), F32),
            pltpu.VMEM((length, LANES), BF16),
            pltpu.SemaphoreType.DMA((5,)),
        ],
        extra=36,
        away=5,
    )


def slot_rows(info, k):
    return pl.ds(pl.multiple_of((info[4, 1] ^ k) * 256, 256), 256)


def attn_out_kernel(plan, info, mix_own, mix_oth, w_own, w_oth, *outs):
    for out, pieces in zip(outs, plan):
        at = 0
        for k, first, count in pieces:
            start = pl.multiple_of((info[4, 1] ^ k) * 256 + first, 128)
            rows = pl.ds(start, count)
            mix = jnp.concatenate([mix_own[rows, :], mix_oth[rows, :]], axis=1)
            for p in range(4):
                weight = jnp.concatenate([w_own[k ^ p, 384:512], w_oth[k ^ p, 384:512]], axis=0)
                out[at : at + count, p * 256 : (p + 1) * 256] = mm(mix, weight, NN).astype(BF16)
            at += count


def relay_kernel(first, x, p0, got, part, sent_out, kept_out):
    half = got.shape[0] // 2
    sent_out[...] = (part[...].astype(F32) + got[half:, :].astype(F32)).astype(BF16)
    rows = slice(first, first + half)
    kept_out[...] = x[rows, :].astype(F32) + p0[rows, :].astype(F32) + got[:half, :].astype(F32)


def middle_kernel(kept_a, got_a, kept_b, got_b, out):
    half = kept_a.shape[0]
    out[:half, :] = (kept_a[...] + got_a[...].astype(F32)).astype(BF16)
    out[half:, :] = (kept_b[...] + got_b[...].astype(F32)).astype(BF16)


def ffn_kernel(k, index, *refs):
    pieces = 2 if k == 3 else 1
    part = jnp.concatenate([ref[...] for ref in refs[:pieces]], axis=0)
    d0, d1, d2, d3, gains, w_own, w_oth, *refs = refs[pieces:]
    backs = refs[-pieces:]
    f0, f1, f2, f3, h_out, hid_out, dug_out, mid_out = refs[-8 - pieces : -pieces]
    parts = [part[:, (k ^ p) * 256 : ((k ^ p) + 1) * 256] for p in range(4)]
    mid_out[...] = parts[0]
    units, _ = moments([v.astype(F32) for v in parts], 4 * 256)
    low = [(units[p] * gains[p, 1:2, :]).astype(BF16) for p in range(4)]
    for p in range(4):
        h_out[:, p * 256 : (p + 1) * 256] = low[p]
    grads = [ref[...] for ref in (d0, d1, d2, d3)]

    def weight(p, i):
        rows = slice(i * 384, (i + 1) * 384)
        return jnp.concatenate([w_own[p, rows], w_oth[p, rows]], axis=0)

    gate = sum(mm(low[p], weight(p, 0), NT) for p in range(4))
    up = sum(mm(low[p], weight(p, 1), NT) for p in range(4))
    dhidden = sum(mm(grads[p], weight(p, 2), NT) for p in range(4))
    phi = 0.5 * (1.0 + lax.erf(gate * (2.0**-0.5)))
    density = jnp.exp(-0.5 * gate * gate) * ((2.0 * math.pi) ** -0.5)
    act = gate * phi
    hidden = (act * up).astype(BF16)
    dgate = (dhidden * up * (phi + gate * density)).astype(BF16)
    dup = (dhidden * act).astype(BF16)
    hid_out[...] = hidden
    dug_out[:, :384] = dgate[:, :384]
    dug_out[:, 384:768] = dup[:, :384]
    dug_out[:, 768:1152] = dgate[:, 384:]
    dug_out[:, 1152:] = dup[:, 384:]
    for p in range(4):
        got = mm(dgate, weight(p, 0), NN) + mm(dup, weight(p, 1), NN)
        got = got.astype(BF16)
        for i, out in enumerate(backs):
            out[:, (k ^ p) * 256 : ((k ^ p) + 1) * 256] = got[i * (256 // pieces) : (i + 1) * (256 // pieces)]
    for p, out in enumerate((f0, f1, f2, f3)):
        out[...] = mm(hidden, weight(p, 2), NN).astype(BF16)


def run_ffn(k, index, mids, grads, gains, w_own, w_oth, held):
    rows = grads[0].shape[0]
    whole = lambda shape: pl.BlockSpec(shape, lambda i, s: (0,) * len(shape))
    block = lambda n: pl.BlockSpec((256, n), lambda i, s: (s[0] ^ k, 0))
    widths = [256] * 4 + [1024, 768, 1536, 256]
    outs = pl.pallas_call(
        functools.partial(ffn_kernel, k),
        grid_spec=pltpu.PrefetchScalarGridSpec(
            num_scalar_prefetch=1,
            grid=(1,),
            in_specs=[whole(v.shape) for v in mids]
            + [block(256)] * 4
            + [whole(gains.shape), whole(w_own.shape), whole(w_oth.shape)]
            + [pl.BlockSpec(memory_space=pl.ANY)] * len(held),
            out_specs=[block(n) for n in widths] + [whole(v.shape) for v in mids],
        ),
        out_shape=[jax.ShapeDtypeStruct((rows, n), BF16) for n in widths]
        + [jax.ShapeDtypeStruct(v.shape, BF16) for v in mids],
        input_output_aliases={8 + len(mids) + i: i for i in range(len(held))},
        compiler_params=room(26),
        cost_estimate=COST,
    )(index, *mids, *grads, gains, w_own, w_oth, *held)
    return outs[:8], list(outs[8:])


def pack_kernel(*refs):
    out = refs[-1]
    planes, _, rows, _ = out.shape
    for p in range(4):
        block = slice(p * 256, (p + 1) * 256)
        total = sum(ref[block, :].astype(F32) for ref in refs[:-1]).astype(BF16)
        for d in range(planes):
            out[d, p] = total[d * rows : (d + 1) * rows]


def pack_dp(*terms):
    planes, width = lax.axis_size("dp"), terms[0].shape[1]
    if planes > 16:
        total = sum(v.astype(F32) for v in terms).astype(BF16)
        return jnp.swapaxes(total.reshape(4, planes, 256 // planes, width), 0, 1)
    return whole_call(
        pack_kernel, [((planes, 4, 256 // planes, width), BF16)], terms, scalars=0
    )[0]


def norm_back(grads, units, inverse, gains):
    scaled = [g * w for g, w in zip(grads, gains)]
    first = sum(jnp.sum(v, axis=1, keepdims=True) for v in scaled) / 1024
    second = sum(jnp.sum(v * u, axis=1, keepdims=True) for v, u in zip(scaled, units)) / 1024
    return [inverse * (v - first - u * second) for v, u in zip(scaled, units)]


def middle_back_kernel(info, mid, p0, p1, p2, p3a, p3b, d0, d1, d2, d3, gains, dx_out, dz_out, gain_out):
    rows = slot_rows(info, 0)
    at = [slice(p * 256, (p + 1) * 256) for p in range(4)]
    units, inverse = moments([mid[:, a].astype(F32) for a in at], 1024)
    last = jnp.concatenate([p3a[...], p3b[...]], axis=0)
    grads = [sum(part[:, a].astype(F32) for part in (p0, p1, p2, last)) for a in at]
    back = norm_back(grads, units, inverse, [gains[p, 1:2, :] for p in range(4)])
    for p, dy in enumerate((d0, d1, d2, d3)):
        total = back[p] + dy[rows, :].astype(F32)
        dx_out[:, at[p]] = total
        dz_out[:, at[p]] = total.astype(BF16)
        gain_out[p : p + 1, :] = jnp.sum(grads[p] * units[p], axis=0, keepdims=True)


def mixed_back_kernel(k, index, *refs):
    pieces = 2 if k == 3 else 1
    part = jnp.concatenate([ref[...] for ref in refs[:pieces]], axis=0)
    w_own, w_oth = refs[pieces : pieces + 2]
    own_out, oth_out, dz_out = refs[-3:]
    total = None
    for p in range(4):
        piece = part[:, (k ^ p) * 256 : ((k ^ p) + 1) * 256]
        dz_out[:, p * 256 : (p + 1) * 256] = piece
        term = mm(piece, jnp.concatenate([w_own[p], w_oth[p]], axis=0), NT)
        total = term if total is None else total + term
    own_out[...] = total[:, :128].astype(BF16)
    oth_out[...] = total[:, 128:].astype(BF16)


def run_mixed_back(k, index, parts, w_own, w_oth, held):
    rows = 4 * 256
    whole = lambda shape: pl.BlockSpec(shape, lambda i, s: (0,) * len(shape))
    block = lambda n: pl.BlockSpec((256, n), lambda i, s: (s[0] ^ k, 0))
    weight = pl.BlockSpec((4, 128, 256), lambda i, s: (0, 3, 0))
    return pl.pallas_call(
        functools.partial(mixed_back_kernel, k),
        grid_spec=pltpu.PrefetchScalarGridSpec(
            num_scalar_prefetch=1,
            grid=(1,),
            in_specs=[whole(v.shape) for v in parts]
            + [weight, weight]
            + [pl.BlockSpec(memory_space=pl.ANY)] * len(held),
            out_specs=[block(128), block(128), block(1024)],
        ),
        out_shape=[jax.ShapeDtypeStruct((rows, n), BF16) for n in (128, 128, 1024)],
        input_output_aliases={3 + len(parts) + i: i for i in range(len(held))},
        compiler_params=room(12),
        cost_estimate=COST,
    )(index, *parts, w_own, w_oth, *held)


def to_row_form(column):
    return jnp.transpose(jnp.broadcast_to(column, (column.shape[0], LANES)))[0:1, :]


def input_back_kernel(d_own, d_oth, w_own, w_oth, h, gains, o0, o1, o2, o3, sums_out, gain_out):
    step = pl.program_id(0)
    grad = jnp.concatenate([d_own[...], d_oth[...]], axis=1)
    first = second = None
    for p, out in enumerate((o0, o1, o2, o3)):
        weight = jnp.concatenate([w_own[p, :384], w_oth[p, :384]], axis=0)
        got = mm(grad, weight, NN)
        out[...] = got.astype(BF16)
        crossed = got * h[:, p * 256 : (p + 1) * 256].astype(F32)
        scaled = got * gains[p, 0:1, :]
        scaled = scaled[:, :128] + scaled[:, 128:]
        across = crossed[:, :128] + crossed[:, 128:]
        first = scaled if first is None else first + scaled
        second = across if second is None else second + across
        part = jnp.sum(crossed, axis=0, keepdims=True) / gains[p, 0:1, :]

        @pl.when(step == 0)
        def _():
            gain_out[p : p + 1, :] = part

        @pl.when(step > 0)
        def _():
            gain_out[p : p + 1, :] += part

    sums_out[0:1, :] = jnp.sum(jnp.transpose(first), axis=0, keepdims=True)
    sums_out[1:2, :] = jnp.sum(jnp.transpose(second), axis=0, keepdims=True)


def run_input_back(d_own, d_oth, w_own, w_oth, h, gains):
    rows = h.shape[0]
    whole = lambda shape: pl.BlockSpec(shape, lambda i: (0,) * len(shape))
    block = lambda n: pl.BlockSpec((512, n), lambda i: (i, 0))
    return pl.pallas_call(
        input_back_kernel,
        grid=(rows // 512,),
        in_specs=[block(384), block(384), whole(w_own.shape), whole(w_oth.shape), block(1024), whole(gains.shape)],
        out_specs=[block(256)] * 4 + [pl.BlockSpec((2, 512), lambda i: (0, i)), whole((4, 256))],
        out_shape=[jax.ShapeDtypeStruct((rows, 256), BF16)] * 4
        + [jax.ShapeDtypeStruct((2, rows), F32), jax.ShapeDtypeStruct((4, 256), F32)],
        compiler_params=room(24),
        cost_estimate=COST,
    )(d_own, d_oth, w_own, w_oth, h, gains)


def input_grad_kernel(p0, p1, p2, p3, sums, h, dz, inv, gains, out):
    first = to_columns(sums[0:1, :]) / 1024
    second = to_columns(sums[1:2, :]) / 1024
    both = lambda v: jnp.concatenate([v, v], axis=1)
    gain = gains[0, 0:1, :]
    total = sum(ref[...].astype(F32) for ref in (p0, p1, p2, p3)) * gain
    unit = h[...].astype(F32) / gain
    out[...] = dz[...].astype(F32) + both(inv[...]) * (total - both(first) - unit * both(second))


def run_input_grad(parts, sums, h, dz, inv, gains):
    rows = h.shape[0]
    block = lambda n: pl.BlockSpec((256, n), lambda i: (i, 0))
    return pl.pallas_call(
        input_grad_kernel,
        grid=(rows // 256,),
        in_specs=[block(256)] * 4
        + [pl.BlockSpec((2, 256), lambda i: (0, i)), block(256), block(256), block(128)]
        + [pl.BlockSpec(gains.shape, lambda i: (0, 0, 0))],
        out_specs=block(256),
        out_shape=jax.ShapeDtypeStruct((rows, 256), F32),
        compiler_params=room(12),
        cost_estimate=COST,
    )(*parts, sums, h, dz, inv, gains)


def adam_update(master, first_moment, second, gradient, factor, decay_rate, step_rate):
    scaled = gradient * factor
    first_new = BETA_ONE * first_moment + (1.0 - BETA_ONE) * scaled
    second_new = BETA_TWO * second + (1.0 - BETA_TWO) * scaled * scaled
    first_hat = first_new / (1.0 - BETA_ONE**STEP)
    second_hat = second_new / (1.0 - BETA_TWO**STEP)
    master_new = master - step_rate * (
        first_hat / (jnp.sqrt(second_hat) + ADAM_EPSILON) + decay_rate * master
    )
    return (first_new, second_new, master_new)


def positions(segment):
    length = segment.shape[0]
    number = jnp.arange(length, dtype=jnp.int32)
    before = jnp.concatenate([segment[:1] - 1, segment[:-1]])
    change_marks = jnp.where(segment != before, number, jnp.zeros_like(number))
    return number - lax.cummax(change_marks, axis=0)


def rope_table(place):
    lane = jnp.arange(LANES) % 64
    frequency = ROPE_BASE ** (-(2.0 * (lane % 32).astype(F32)) / 64)
    turned = place.astype(F32)[:, None] * frequency[None, :]
    return jnp.where(lane[None, :] < 32, jnp.cos(turned), jnp.sin(turned))


def on_device(
    tokens, segment_ids, cotangent, qkv_weight, attn_weight, in_weight, out_weight, norm_gains,
    qkv_master, attn_master, in_master, out_master,
    qkv_first, attn_first, in_first, out_first,
    qkv_second, attn_second, in_second, out_second,
    gains_first, gains_second,
):
    col, row = lax.axis_index("col"), lax.axis_index("row")
    segment = segment_ids[0]
    length = segment.shape[0]
    rows = length // 2
    blocks = length // BLOCK
    ff_here = in_weight.shape[2] // 4
    ff_pad = -ff_here % FF_PAD
    ff_wide = ff_here + ff_pad

    qkv_t = jnp.transpose(qkv_weight, (1, 2, 3, 0))
    attn_t = attn_weight.reshape(4, LANES, 256)
    in_t = jnp.transpose(in_weight, (1, 2, 0)).reshape(2, 4, ff_here, 256)
    out_t = out_weight.reshape(4, ff_here, 256)

    index = jnp.stack([col, row])
    a = to_col(tokens, 1)
    b = to_col(tokens, 2)
    high = norm_gains.astype(BF16)
    rest = norm_gains - high.astype(F32)
    middle = rest.astype(BF16)
    lowest = (rest - middle.astype(F32)).astype(BF16)
    gain_rows = jnp.concatenate([high, middle, lowest, jnp.zeros((10, 256), BF16)], axis=0)
    gain_rows = lax.optimization_barrier(gain_rows)

    def wide_piece(k):
        qkv = lax.dynamic_slice_in_dim(qkv_t, 2 * (col ^ k), 2, 1).reshape(3 * LANES, 256)
        return jnp.concatenate(
            [qkv, lax.dynamic_index_in_dim(attn_t, col ^ k, 0, keepdims=False), gain_rows], axis=0
        )

    half = tokens.shape[0] // 2
    x3a, x3b = to_col(a[:half], 2), to_col(b[half:], 1)
    xs = [tokens, a, b, x3a, x3b]
    wa_parts = exchange_col([wide_piece(k) for k in range(4)])
    wa_own = jnp.stack(after(wa_parts, x3a, x3b))
    ff_gate = (x3a, x3b)
    gains = wa_own[:, 512:518].astype(F32).reshape(4, 3, 2, 256)
    gains = gains[:, 0] + gains[:, 1] + gains[:, 2]

    planes = lax.axis_size("dp")
    fill = [(0, 0), (0, 0), (0, ff_pad), (0, 0)]
    ff_t = jnp.pad(jnp.concatenate([in_t, out_t[None]], axis=0), fill)
    ff_t = ff_t.reshape(3, 4, planes, ff_wide // planes, 256)
    ff_t = lax.dynamic_index_in_dim(ff_t, lax.axis_index("dp"), 2, keepdims=False)
    ff_parts = [lax.dynamic_index_in_dim(ff_t, col ^ k, 1, keepdims=False) for k in range(4)]
    ff_parts = exchange_col(after(ff_parts, *ff_gate))
    first = segment[::BLOCK]
    last = segment[BLOCK - 1 :: BLOCK]
    low = jnp.sum((segment[None, :] < first[:, None]).astype(jnp.int32), axis=1) // BLOCK
    high = (
        jnp.sum((segment[None, :] <= last[:, None]).astype(jnp.int32), axis=1) + BLOCK - 1
    ) // BLOCK
    place_here = jnp.zeros((blocks,), jnp.int32).at[0].set(row).at[1].set(col)
    info = jnp.stack([low, high, first, last, place_here])
    seg_row = segment_ids.astype(F32)
    table = rope_table(positions(segment))
    own, h1, inv, x_slot = run_qkv(index, xs, gains, wa_own, table)
    h1_recv = to_row(h1)
    dys = exchange_col([after(cotangent, own)] * 4)
    wa_oth = to_row(after(wa_own, own))
    ff_own = lax.all_gather(jnp.stack(after(ff_parts, own)), "dp", axis=2)
    recv = run_away(index, h1_recv, wa_own, table)
    mix_own, mix_away, lse = run_attend(info, own, recv, seg_row)
    mix_own, mix_away, lse, dys, wa_oth = after((mix_own, mix_away, lse, dys, wa_oth), wa_oth)
    mix_oth = to_row(mix_away)
    def attn_out(*plan):
        return whole_call(
            functools.partial(attn_out_kernel, plan),
            [((sum(count for _, _, count in pieces), 1024), BF16) for pieces in plan],
            (info, mix_own, mix_oth, wa_own, wa_oth),
        )

    x_first, y_first = attn_out(((1, 0, 128), (3, 0, 128)), ((2, 128, 128), (3, 128, 128)))
    x_first, y_first = to_col(x_first, 1), to_col(y_first, 2)
    x_part, y_part, part = attn_out(((1, 128, 128),), ((2, 0, 128),), ((0, 0, 256),))
    relay = lambda first, got, mine: whole_call(
        functools.partial(relay_kernel, first),
        [((128, 1024), BF16), ((128, 1024), F32)],
        (x_slot, part, got, mine),
        scalars=0,
    )
    y_second, kept_a = relay(0, x_first, y_part)
    x_second, kept_b = relay(128, y_first, x_part)
    y_second, x_second = to_col(y_second, 2), to_col(x_second, 1)
    (middle,) = whole_call(
        middle_kernel, [((256, 1024), BF16)], (kept_a, y_second, kept_b, x_second), scalars=0
    )
    ff_own = after(ff_own, x_second, y_second).reshape(4, 3 * ff_wide, 256)
    ff_oth = to_row(ff_own)
    m1, m2 = to_col(middle, 1), to_col(middle, 2)
    held, backward = (), [None] * 4
    for k in range(4):
        if k == 1:
            r1, r2 = after((m1, m2), held[0])
            m3a, m3b = to_col(r1[:128], 2), to_col(r2[128:], 1)
        mids = ((middle,), (m1,), (m2,), (m3a, m3b))[k] if k else (middle,)
        held, part = run_ffn(k, index, mids, dys, gains, ff_own, ff_oth, held)
        if k == 1:
            part, m2 = after((part, m2), m3a, m3b)
        backward[k] = [to_col(v, k) for v in part] if k else part
    forward = held[:4]
    h2, hidden, dug, mid_here = held[4:]
    dx_mid, dz, gain_two = whole_call(
        middle_back_kernel,
        [((256, 1024), F32), ((256, 1024), BF16), ((4, 256), F32)],
        (info, middle, *sum(backward, []), *dys, gains),
    )
    z1, z2 = to_col(dz, 1), to_col(dz, 2)
    z3a, z3b = to_col(z1[:128], 2), to_col(z2[128:], 1)

    h2, hidden, dug = after((h2, hidden, dug), z1, z2)
    dy_all = jnp.concatenate(dys, axis=1)
    ffn_own, ffn_oth = (
        jnp.concatenate(
            [
                mm(h2, dug[:, i * 2 * ff_wide : (i + 1) * 2 * ff_wide], TN).astype(BF16),
                mm(dy_all, hidden[:, i * ff_wide : (i + 1) * ff_wide], TN).astype(BF16),
            ],
            axis=1,
        )
        for i in range(2)
    )
    ffn_oth = to_row(ffn_oth)
    ffn_oth, z3a, z3b = after((ffn_oth, z3a, z3b), z3a, z3b)
    ffn_grad = lax.psum_scatter(pack_dp(ffn_own, ffn_oth), "dp", scatter_dimension=0).astype(F32)

    held = ()
    for k, parts in enumerate(((dz,), (z1,), (z2,), (z3a, z3b))):
        held = run_mixed_back(k, index, parts, wa_own, wa_oth, held)
    dm_own, dm_away, dz_here = held
    dm_recv = to_row(dm_away)
    forward = exchange_col(after(forward, dm_own))
    dq_own, dq_away = run_attend_back(
        info, own, recv, seg_row, lse, mix_own, mix_away, dm_own, dm_recv, table
    )
    dq_own, dq_away, forward, dz_here = after((dq_own, dq_away, forward, dz_here), forward[1:])
    layer_out = (mid_here.astype(F32) + sum(v.astype(F32) for v in forward)).astype(BF16)
    dq_oth = to_row(dq_away)

    attn_both = mm(dz_here, jnp.concatenate([mix_own, mix_oth], axis=1), TN)
    attn_sent = to_row(attn_both[:, LANES:].astype(BF16))
    attn_sum = (attn_both[:, :LANES] + attn_sent.astype(F32)).astype(BF16)
    qkv_sum = (mm(h1, dq_own, TN) + mm(h1_recv, dq_away, TN)).astype(BF16)

    *partial_first, sums, gain_one = run_input_back(dq_own, dq_oth, wa_own, wa_oth, h1, gains)
    notes = [
        jnp.concatenate([sums, jnp.pad(jnp.stack([gain_one[k], gain_two[k]]), [(0, 0), (0, rows - 256)])])
        for k in range(4)
    ]
    late = after(pack_dp(jnp.concatenate([qkv_sum, attn_sum], axis=1)), gain_one)
    late = scatter_dp(late)
    notes = exchange_col(notes)
    partial_first = exchange_col(after(partial_first, notes[1]))
    note = sum(notes)
    input_grad = run_input_grad(partial_first, note[:2], h1, dz_here, inv, gains)

    early = ffn_grad.astype(BF16)
    early = natural(exchange_col([early[k] for k in range(4)]), col)
    late = after(late, *partial_first[1:])
    squares = jnp.sum(ffn_grad * ffn_grad) + jnp.sum(late * late)
    message = jnp.concatenate([note[2:, :256], jnp.full((6, 256), squares)], axis=0)
    message = sum_dp(message)
    message = message + to_row(message)
    gain_grad = message[:2]
    total = message[2:3, :LANES] + jnp.sum(gain_grad * gain_grad)
    total = jnp.broadcast_to(total, (8, LANES))
    total, early = after((total, early), *early)
    total = sum(exchange_col([total] * 4))
    grad_norm = jnp.sqrt(total[0, 0])
    factor = CLIP_NORM / (grad_norm + 1e-06)

    shard = late.shape[1]
    late = late.astype(BF16)
    late = natural(exchange_col([late[k] for k in range(4)]), col)
    grad_qkv = jnp.stack([v[:, : 3 * LANES].reshape(shard, 3, 2, 64) for v in late], axis=2).reshape(
        qkv_master.shape
    )
    grad_attn = jnp.concatenate([v[:, 3 * LANES :] for v in late], axis=1).T.reshape(
        attn_master.shape
    )
    grad_in = jnp.stack(
        [
            jnp.concatenate([v[:, i * ff_wide : i * ff_wide + ff_here] for v in early], axis=1)
            for i in range(2)
        ],
        axis=1,
    )
    grad_out = jnp.concatenate([v[:, 2 * ff_wide : 2 * ff_wide + ff_here] for v in early], axis=1).T

    grad_qkv, grad_attn, grad_in, grad_out = (
        v.astype(F32) for v in (grad_qkv, grad_attn, grad_in, grad_out)
    )
    qkv_new = adam_update(
        qkv_master, qkv_first, qkv_second, grad_qkv, factor, WEIGHT_DECAY, LEARN_RATE
    )
    attn_new = adam_update(
        attn_master, attn_first, attn_second, grad_attn, factor, WEIGHT_DECAY, LEARN_RATE
    )
    in_new = adam_update(in_master, in_first, in_second, grad_in, factor, WEIGHT_DECAY, LEARN_RATE)
    out_new = adam_update(
        out_master, out_first, out_second, grad_out, factor, WEIGHT_DECAY, LEARN_RATE
    )
    gains_new = adam_update(
        norm_gains, gains_first, gains_second, gain_grad, factor, 0.0, GAIN_RATE
    )
    return (
        layer_out, input_grad, grad_norm,
        qkv_new[0], attn_new[0], in_new[0], out_new[0],
        qkv_new[1], attn_new[1], in_new[1], out_new[1],
        qkv_new[2], attn_new[2], in_new[2], out_new[2],
        qkv_new[2].astype(BF16), attn_new[2].astype(BF16),
        in_new[2].astype(BF16), out_new[2].astype(BF16),
        gains_new[0], gains_new[1], gains_new[2],
    )


def solution(mesh):
    activations = P(("dp", "row"), "col")
    gains = P(None, "col")
    weights = (
        P("col", None, "row", None), P("row", None, "col"), P("col", None, "row"), P("row", "col"),
    )
    states = (
        P(("col", "dp"), None, "row", None), P("row", None, ("col", "dp")),
        P(("col", "dp"), None, "row"), P("row", ("col", "dp")),
    )
    return jax.shard_map(
        on_device,
        mesh=mesh,
        in_specs=(activations, P("dp", None), activations, *weights, gains)
        + states * 3
        + (gains, gains),
        out_specs=(activations, activations, P()) + states * 4 + (gains, gains, gains),
        check_vma=False,
    )
```
